32 devices in a mesh: inst: 16 (over z, y, core), tp: 2 (over x).
Axes of the slice: x: 2, y: 2, z: 4, core: 2. Of those that a mesh axis runs over, the one named last changes fastest.
Arguments:
- new_pages: bfloat16 [256, 8, 128, 256], P(('inst', 'tp')), may hold values from -6 to 6
- routes: int32 [256], P('inst'), may hold values from 0 to 15, as said below
- resident: bfloat16 [128, 8, 128, 256], P('inst', 'tp'), may hold values from -8 to 8
- queries: bfloat16 [512, 8, 5, 128], P('inst', 'tp'), may hold values from -24 to 24
- own_kv: bfloat16 [512, 8, 256], P('inst', 'tp'), may hold values from -6 to 6
- tables: int32 [512, 16], P('inst'), may hold values from 0 to 39, as said below
- lengths: int32 [512], P('inst'), may hold values from 128 to 2048, as said below
Outputs:
- attention: bfloat16 [512, 8, 5, 128], P('inst', 'tp')
The draws below stay inside these ranges and needn't reach their ends.
Inputs may be any that keep to these rules, and one draw needn't show every extreme that they name: `routes`: each instance sends at most 2 of its 16 new pages to any one instance, and exactly 2 to some instance; in every draw one instance receives 2 pages from every instance. `tables`: entry 0 of every table is pool page 0, a prefix shared by the instance's requests. An entry below 8 names a resident page; entry 8 + i * 2 + c names the page with copy number c that instance i sends to this instance, and only pages that are sent are named. `lengths`: every instance has a request of the greatest length.
All inputs are finite; a program needn't handle non-finite values.
Results may differ from the reference program's by a relative error of at most 0.0044.
Values may be sent and summed in bfloat16 or wider, within the bound.
No kernel may reach another device: no remote copies, remote signals or barrier semaphores. Data moves between devices by JAX's collectives and lax.ppermute only.
A program may use at most 128 MiB of HBM per device.

```python
import jax
import jax.numpy as jnp
from jax import lax

KVH = 8
HD = 128
PAGE = 128
CAP = 2
MAXP = 16
RES = 8
R_DEV = 32
GRP = 5
NPG = 16
REQS = 512
N_INST = 16


def route_plan(key):
    subkeys = jax.random.split(jax.random.fold_in(key, 101), 4)
    hot_order = jax.random.permutation(subkeys[0], N_INST)
    hot_level = jnp.where(hot_order == 0, 2, jnp.where(hot_order < N_INST // 8, 1, 0)).astype(jnp.int32)
    noise_draw = jax.random.randint(subkeys[1], (N_INST, N_INST), 0, N_INST)
    scores = (noise_draw + N_INST * hot_level[None, :]) * N_INST + jnp.arange(N_INST, dtype=jnp.int32)[None, :]
    _, chosen = lax.top_k(scores, NPG)
    paired = jax.random.randint(subkeys[2], (N_INST, NPG // 2), 0, 2)
    paired = paired.at[:, 0].set(1)
    singles = 1 - paired
    first_group = jnp.arange(NPG // 2, dtype=jnp.int32)[None, :] + jnp.cumsum(singles, axis=1) - singles
    second_group = first_group + singles
    group_index = jnp.stack([first_group, second_group], axis=2).reshape(N_INST, NPG)
    destination = jnp.take_along_axis(chosen, group_index, axis=1)
    shuffle = jnp.argsort(jax.random.randint(subkeys[3], (N_INST, NPG), 0, 1 << 20) * NPG + jnp.arange(NPG, dtype=jnp.int32)[None, :], axis=1)
    destination = jnp.take_along_axis(destination, shuffle, axis=1)
    return destination.astype(jnp.int32)


def draw_routes(key, part):
    destination = route_plan(key)
    return destination.reshape(N_INST * NPG).astype(jnp.int32)


def draw_tables(key, part):
    destination = route_plan(key)
    key = jax.random.fold_in(key, 41)
    same_dest = destination[:, :, None] == destination[:, None, :]
    earlier = jnp.arange(NPG, dtype=jnp.int32)[None, :] < jnp.arange(NPG, dtype=jnp.int32)[:, None]
    copy_rank = jnp.sum(jnp.where(same_dest & earlier[None], 1, 0), axis=2).astype(jnp.int32)
    senders = jnp.broadcast_to(jnp.arange(N_INST, dtype=jnp.int32)[:, None], (N_INST, NPG))
    filled = jnp.zeros((N_INST, N_INST, CAP), jnp.int32).at[destination, senders, copy_rank].set(1)
    usable_slot = jnp.concatenate([jnp.ones((N_INST, RES), jnp.int32), filled.reshape(N_INST, N_INST * CAP)], axis=1)
    counts = jnp.sum(usable_slot, axis=1)
    drawn_picks = jax.random.randint(key, (N_INST, R_DEV, MAXP), 0, 1 << 24) % counts[:, None, None]
    cumulative = jnp.cumsum(usable_slot, axis=1)
    slot_index = jnp.sum(jnp.where(cumulative[:, None, None, :] <= drawn_picks[..., None], 1, 0), axis=3).astype(jnp.int32)
    slot_index = slot_index.at[:, :, 0].set(0)
    return slot_index.reshape(N_INST * R_DEV, MAXP).astype(jnp.int32)


def draw_lengths(key, part):
    key = jax.random.fold_in(key, 53)
    key_shift, key_extra = jax.random.split(key)
    shifts = jax.random.randint(key_shift, (N_INST, R_DEV), 0, 4)
    span_limit = jnp.right_shift(jnp.full((N_INST, R_DEV), (MAXP - 1) * PAGE, jnp.int32), shifts)
    extra_tokens = jax.random.randint(key_extra, (N_INST, R_DEV), 0, 1 << 24) % (span_limit + 1)
    drawn_lengths = PAGE + extra_tokens
    drawn_lengths = drawn_lengths.at[:, 0].set(MAXP * PAGE)
    return drawn_lengths.reshape(N_INST * R_DEV).astype(jnp.int32)


def draw_queries(key, part):
    key = jax.random.fold_in(key, 11)
    full_shape = (N_INST * R_DEV, KVH, GRP, HD)
    values_drawn = jnp.clip(jax.random.normal(key, full_shape, jnp.float32), -6.0, 6.0)
    return values_drawn.astype(jnp.bfloat16)


def draw_resident(key, part):
    key = jax.random.fold_in(key, 23)
    full_shape = (N_INST * RES, KVH, PAGE, 2 * HD)
    values_drawn = jnp.clip(jax.random.normal(key, full_shape, jnp.float32), -6.0, 6.0)
    return values_drawn.astype(jnp.bfloat16)


def block_levels(rng, extent, pieces, low, high):
    gain, own = 1.0, jax.random.fold_in(rng, 6)
    for dim, shards_of in pieces:
        draws = jnp.exp(jax.random.uniform(jax.random.fold_in(own, dim), (shards_of,), jnp.float32, low / len(pieces), high / len(pieces)))
        gain = gain * jnp.repeat(draws, extent[dim] // shards_of).reshape([-1 if axis == dim else 1 for axis in range(len(extent))])
    return gain


def gaussian(key, shape, spread, most, pieces=(), kind=jnp.bfloat16):
    values = jax.random.normal(key, shape, jnp.float32) * spread
    if len(pieces) > 0:
        values = block_levels(key, shape, pieces, -0.22, 0.18) * values
    return jnp.clip(values, min=-most, max=most).astype(kind)


def setup_inputs(seed: int = 0) -> dict:
    arg_keys = jax.random.split(jax.random.key(seed), 8)
    return {
        "new_pages": gaussian(arg_keys[0], (N_INST * NPG, KVH, PAGE, 2 * HD), 1.0, 6.0, ((0, 32),)),
        "routes": draw_routes(jax.random.fold_in(arg_keys[7], 71), 0),
        "resident": draw_resident(jax.random.fold_in(arg_keys[7], 71), 0),
        "queries": draw_queries(jax.random.fold_in(arg_keys[7], 71), 0),
        "own_kv": gaussian(arg_keys[4], (REQS, KVH, 2 * HD), 1.0, 6.0, ((0, 16), (1, 2))),
        "tables": draw_tables(jax.random.fold_in(arg_keys[7], 71), 0),
        "lengths": draw_lengths(jax.random.fold_in(arg_keys[7], 71), 0),
    }


def arrival_ranks(routes):
    destination = routes.reshape(N_INST, NPG)
    same_dest = destination[:, :, None] == destination[:, None, :]
    earlier = jnp.arange(NPG, dtype=jnp.int32)[None, :] < jnp.arange(NPG, dtype=jnp.int32)[:, None]
    copy_rank = jnp.sum(jnp.where(same_dest & earlier[None], 1, 0), axis=2).astype(jnp.int32)
    return destination, copy_rank


def one_request(query, own_pair, table, length, page_pool):
    head_dim = query.shape[-1]
    scaling = head_dim ** -0.5
    pages = page_pool[table]
    keys = pages[..., :head_dim].astype(jnp.float32)
    values = pages[..., head_dim:].astype(jnp.float32)
    query_wide = query.astype(jnp.float32)
    raw_scores = jnp.einsum("hqd,mhpd->hqmp", query_wide, keys) * scaling
    own_keys = own_pair[:, :head_dim].astype(jnp.float32)
    own_values = own_pair[:, head_dim:].astype(jnp.float32)
    own_scores = jnp.einsum("hqd,hd->hq", query_wide, own_keys) * scaling
    page_count, page_width = raw_scores.shape[2], raw_scores.shape[3]
    places = lax.broadcasted_iota(jnp.int32, (page_count, page_width), 0) * page_width + lax.broadcasted_iota(jnp.int32, (page_count, page_width), 1)
    usable = places < length
    masked = jnp.where(usable[None, None], raw_scores, -jnp.inf)
    highest = jnp.maximum(jnp.max(masked, axis=(2, 3)), own_scores)
    exponent = jnp.exp(masked - highest[..., None, None])
    own_exponent = jnp.exp(own_scores - highest)
    totals = jnp.sum(exponent, axis=(2, 3)) + own_exponent
    weights = exponent.astype(jnp.bfloat16).astype(jnp.float32)
    own_weights = own_exponent.astype(jnp.bfloat16).astype(jnp.float32)
    mixture = jnp.einsum("hqmp,mhpd->hqd", weights, values)
    mixture = mixture + own_weights[..., None] * own_values[:, None, :]
    return (mixture / totals[..., None]).astype(jnp.bfloat16)


def reference(new_pages, routes, resident, queries, own_kv, tables, lengths):
    destination, copy_rank = arrival_ranks(routes)
    shaped_new = new_pages.reshape((N_INST, NPG) + new_pages.shape[1:])
    shaped_res = resident.reshape((N_INST, RES) + resident.shape[1:])
    shaped_queries = queries.reshape((N_INST, R_DEV) + queries.shape[1:])
    shaped_pairs = own_kv.reshape((N_INST, R_DEV) + own_kv.shape[1:])
    shaped_tables = tables.reshape(N_INST, R_DEV, MAXP)
    shaped_lengths = lengths.reshape(N_INST, R_DEV)
    sources = jnp.arange(N_INST, dtype=jnp.int32)
    positions = jnp.arange(NPG, dtype=jnp.int32)
    copies = jnp.arange(CAP, dtype=jnp.int32)

    def one_instance(items):
        target, res_pages, query_rows, pair_rows, table_rows, length_rows = items
        matched = (destination[:, None, :] == target) & (copy_rank[:, None, :] == copies[None, :, None])
        picked = jnp.sum(jnp.where(matched, positions[None, None, :], 0), axis=2).astype(jnp.int32)
        filled = jnp.any(matched, axis=2)
        arrived = shaped_new[sources[:, None], picked]
        arrived = jnp.where(filled[:, :, None, None, None], arrived, jnp.zeros((), arrived.dtype))
        page_pool = jnp.concatenate([res_pages, arrived.reshape((N_INST * CAP,) + arrived.shape[2:])], axis=0)

        def per_request(row):
            return one_request(row[0], row[1], row[2], row[3], page_pool)

        return lax.map(per_request, (query_rows, pair_rows, table_rows, length_rows))

    result = lax.map(one_instance, (sources, shaped_res, shaped_queries, shaped_pairs, shaped_tables, shaped_lengths))
    return result.reshape(queries.shape)
```

```python
import functools

import jax
import jax.numpy as jnp
from jax import lax
from jax.experimental import pallas as pl
from jax.experimental.pallas import tpu as pltpu
from jax.sharding import PartitionSpec as P

CAP = 2
LANES = 128
NEG = -1e30
VMEM_LIMIT = 56 * 1024 * 1024


def tail_rows(blocks, per_block):
    return -(-3 * blocks * per_block // 16) * 16


class Layout:
    def __init__(self, groups, requests):
        self.groups = groups
        self.requests = requests
        self.rows = groups * requests
        self.per_row = LANES // requests
        self.lse_rows = -(-groups // self.per_row)

    def parcel(self, blocks):
        return blocks * self.rows + tail_rows(blocks, self.lse_rows)

    def lane_masks(self):
        lane = lax.broadcasted_iota(jnp.int32, (self.requests, LANES), 1)
        row = lax.broadcasted_iota(jnp.int32, (self.requests, LANES), 0)
        return [lane == row + quarter * self.requests for quarter in range(self.per_row)]

    def column_to_rows(self, column, masks):
        out = []
        for line in range(self.lse_rows):
            total = None
            for quarter in range(self.per_row):
                g = line * self.per_row + quarter
                if g < self.groups:
                    part = column[g * self.requests : (g + 1) * self.requests]
                    part = jnp.where(masks[quarter], part, 0.0)
                    total = part if total is None else total + part
            out.append(jnp.sum(total, axis=0, keepdims=True))
        return out

    def row_to_column(self, line, quarter, masks):
        wide = jnp.broadcast_to(line, (self.requests, LANES))
        return jnp.sum(jnp.where(masks[quarter], wide, 0.0), axis=1, keepdims=True)


def store_tail(out, first, lse, tail):
    count = lse.shape[0]
    tail[...] = jnp.zeros_like(tail)
    high = lse.astype(jnp.bfloat16).astype(jnp.float32)
    middle = (lse - high).astype(jnp.bfloat16).astype(jnp.float32)
    tail[0:count] = high
    tail[count : 2 * count] = middle
    tail[2 * count : 3 * count] = lse - high - middle
    out[first : first + tail.shape[0]] = tail[...].astype(jnp.bfloat16)


def load_tail(ref, first, count, tail):
    tail[...] = ref[first : first + tail.shape[0]].astype(jnp.float32)
    return tail[0:count] + tail[count : 2 * count] + tail[2 * count : 3 * count]


def attend_kernel(shape, lay, lists, *refs):
    (na, nb, nt, order, width) = shape
    q_refs, refs = refs[: nt if order == "b" else nb], refs[nt if order == "b" else nb :]
    meta, own_pages, other_pages = refs[:3]
    outs = refs[3 : 3 + len(q_refs)]
    bias, acc, top, total, lse = refs[3 + len(q_refs) : 8 + len(q_refs)]
    tail = refs[8 + len(q_refs)]
    rows, head_dim = lay.rows, own_pages.shape[-1] // 2
    page = own_pages.shape[-2]
    scaling = head_dim ** (-0.5)
    dests = na * nb
    masks = lay.lane_masks()
    lane = lax.broadcasted_iota(jnp.int32, (lay.requests, LANES), 1)
    position = lax.broadcasted_iota(jnp.int32, (lay.requests, page), 1)

    def column_of(dest, index):
        plane = meta[dest, pl.ds(pl.multiple_of(index // LANES * lay.requests, lay.requests), lay.requests)]
        picked = jnp.where(lane == index % LANES, plane.astype(jnp.float32), 0.0)
        return jnp.sum(picked, axis=1, keepdims=True)

    def place(sb, sa, st):
        if order == "b":
            return st, sb * na + sa
        return sb, st * na + sa

    for sb in range(nb):

        def one_dest(sa, carry, sb=sb):
            dest = sb * na + sa
            entry = dest * 5
            count_own = lists[entry]
            count_other = lists[5 * dests + entry]

            @pl.when(count_own + count_other == 0)
            def _():
                for st in range(nt):
                    which, block = place(sb, sa, st)
                    outs[which][pl.ds(pl.multiple_of(block * rows, rows), rows)] = jnp.zeros(
                        (rows, head_dim), jnp.bfloat16
                    )
                    lse[which, pl.ds(block * lay.lse_rows, lay.lse_rows)] = jnp.full(
                        (lay.lse_rows, LANES), NEG, jnp.float32
                    )

            @pl.when(count_own + count_other > 0)
            def _():
                acc[...] = jnp.zeros_like(acc)
                total[...] = jnp.zeros_like(total)
                top[...] = jnp.full_like(top, 2 * NEG)
                for source, (pages, count) in enumerate(
                    ((own_pages, count_own), (other_pages, count_other))
                ):

                    def one_page(j, carry, source=source, pages=pages):
                        base = source * 5 * dests + entry
                        index = lists[base + 1 + j]
                        column = lists[base + 3 + j]
                        full = column_of(dest, column)
                        part = column_of(dest, width + column)
                        times = full + jnp.where(position < part.astype(jnp.int32), 1.0, 0.0)
                        bias[...] = jnp.where(times > 0, jnp.log(jnp.maximum(times, 1.0)), NEG)
                        for st in range(nt):
                            which, block = place(sb, sa, st)
                            if order == "b":
                                query = q_refs[st][dest]
                            else:
                                query = q_refs[sb][block]
                            head = lists[10 * dests + st]
                            keys = pages[index, head, 0, :, :head_dim]
                            values = pages[index, head, 0, :, head_dim:]
                            scores = lax.dot_general(
                                query, keys, (((1,), (1,)), ((), ())),
                                preferred_element_type=jnp.float32,
                            )
                            scores = scores * scaling
                            scores = scores + jnp.concatenate([bias[...]] * lay.groups, axis=0)
                            before = top[st]
                            now = jnp.maximum(before, jnp.max(scores, axis=1, keepdims=True))
                            shrink = jnp.exp(before - now)
                            weights = jnp.exp(scores - now)
                            total[st] = total[st] * shrink + jnp.sum(weights, axis=1, keepdims=True)
                            acc[st] = acc[st] * shrink + jnp.dot(
                                weights.astype(jnp.bfloat16), values,
                                preferred_element_type=jnp.float32,
                            )
                            top[st] = now
                        return carry

                    lax.fori_loop(0, count, one_page, 0)
                for st in range(nt):
                    which, block = place(sb, sa, st)
                    outs[which][pl.ds(pl.multiple_of(block * rows, rows), rows)] = (
                        acc[st] / total[st]
                    ).astype(jnp.bfloat16)
                    lines = lay.column_to_rows(top[st] + jnp.log(total[st]), masks)
                    for number, line in enumerate(lines):
                        lse[which, pl.ds(block * lay.lse_rows + number, 1)] = line

            return carry

        lax.fori_loop(0, na, one_dest, 0)
    for which, out in enumerate(outs):
        store_tail(out, out.shape[0] - tail.shape[0], lse[which], tail)


def merge_kernel(n, blocks, parts, lay, *refs):
    ins, outs = refs[:n], refs[n : n + parts]
    weights, merged, tail_in, tail_out = refs[n + parts :]
    lines = blocks * lay.lse_rows
    each = blocks // parts
    masks = lay.lane_masks()
    parts_lse = [load_tail(ref, blocks * lay.rows, lines, tail_in) for ref in ins]
    highest = functools.reduce(jnp.maximum, parts_lse)
    exps = [jnp.exp(value - highest) for value in parts_lse]
    total = functools.reduce(jnp.add, exps)
    for i in range(n):
        weights[i] = exps[i] / total
    merged[...] = highest + jnp.log(total)
    for which in range(parts):

        def one_block(b, carry, which=which):
            source = which * each + b
            for g in range(lay.groups):
                line = source * lay.lse_rows + g // lay.per_row
                start = pl.multiple_of(source * lay.rows, lay.rows) + g * lay.requests
                mixed = None
                for i in range(n):
                    column = lay.row_to_column(weights[i, pl.ds(line, 1)], g % lay.per_row, masks)
                    term = column * ins[i][pl.ds(start, lay.requests)].astype(jnp.float32)
                    mixed = term if mixed is None else mixed + term
                goal = pl.multiple_of(b * lay.rows, lay.rows) + g * lay.requests
                outs[which][pl.ds(goal, lay.requests)] = mixed.astype(jnp.bfloat16)
            return carry

        lax.fori_loop(0, each, one_block, 0)
        span = each * lay.lse_rows
        store_tail(outs[which], each * lay.rows, merged[which * span : (which + 1) * span], tail_out)


def resident_kernel(lay, q_ref, pages, own, meta, out, lse, scores):
    heads, count, page = q_ref.shape[0], pages.shape[0], pages.shape[2]
    head_dim = pages.shape[-1] // 2
    scaling = head_dim ** (-0.5)
    masks = lay.lane_masks()
    position = lax.broadcasted_iota(jnp.int32, (lay.requests, page), 1)
    lane = lax.broadcasted_iota(jnp.int32, (lay.requests, LANES), 1)
    plane = meta[...].astype(jnp.float32)

    def column_of(index):
        return jnp.sum(jnp.where(lane == index, plane, 0.0), axis=1, keepdims=True)

    biases = []
    for p in range(count):
        part = column_of(count + p).astype(jnp.int32)
        times = column_of(p) + jnp.where(position < part, 1.0, 0.0)
        biases.append(jnp.where(times > 0, jnp.log(jnp.maximum(times, 1.0)), NEG))
    lse[...] = jnp.zeros_like(lse)
    for h in range(heads):
        query = q_ref[h]
        own_keys = jnp.concatenate([own[h, :, :head_dim].astype(jnp.float32)] * lay.groups, axis=0)
        own_values = jnp.concatenate([own[h, :, head_dim:].astype(jnp.float32)] * lay.groups, axis=0)
        own_scores = jnp.sum(query.astype(jnp.float32) * own_keys, axis=1, keepdims=True) * scaling
        highest = jnp.broadcast_to(own_scores, (lay.rows, page))
        for p in range(count):
            value = lax.dot_general(
                query, pages[p, h, :, :head_dim], (((1,), (1,)), ((), ())),
                preferred_element_type=jnp.float32,
            )
            value = value * scaling + jnp.concatenate([biases[p]] * lay.groups, axis=0)
            scores[p] = value
            highest = jnp.maximum(highest, value)
        highest = jnp.max(highest, axis=1, keepdims=True)
        own_weights = jnp.exp(own_scores - highest)
        total = jnp.zeros((lay.rows, page), jnp.float32)
        mixed = own_weights * own_values
        for p in range(count):
            weights = jnp.exp(scores[p] - highest)
            total = total + weights
            mixed = mixed + jnp.dot(
                weights.astype(jnp.bfloat16), pages[p, h, :, head_dim:],
                preferred_element_type=jnp.float32,
            )
        total = jnp.sum(total, axis=1, keepdims=True) + own_weights
        out[h] = mixed / total
        column = jnp.broadcast_to(highest + jnp.log(total), (lay.rows, LANES))
        for number, line in enumerate(lay.column_to_rows(column, masks)):
            at = h * lay.lse_rows + number
            lse[at : at + 1] = line


def final_kernel(n, heads, lay, *refs):
    ins, refs = refs[: n * heads], refs[n * heads :]
    local, local_lse, out, weights, tail = refs
    masks = lay.lane_masks()
    for h in range(heads):
        parcels = ins[h * n : (h + 1) * n]
        parts = [load_tail(ref, lay.rows, lay.lse_rows, tail) for ref in parcels]
        parts.append(local_lse[h * lay.lse_rows : (h + 1) * lay.lse_rows])
        highest = functools.reduce(jnp.maximum, parts)
        exps = [jnp.exp(value - highest) for value in parts]
        total = functools.reduce(jnp.add, exps)
        for i in range(n + 1):
            weights[i] = exps[i] / total
        for g in range(lay.groups):
            line, quarter = g // lay.per_row, g % lay.per_row
            span = slice(g * lay.requests, (g + 1) * lay.requests)
            mixed = lay.row_to_column(weights[n, line : line + 1], quarter, masks) * local[h, span]
            for i in range(n):
                column = lay.row_to_column(weights[i, line : line + 1], quarter, masks)
                mixed = mixed + column * parcels[i][span].astype(jnp.float32)
            out[h, span] = mixed.astype(out.dtype)


def vmem(count):
    return [pl.BlockSpec(memory_space=pltpu.VMEM)] * count


def params():
    return pltpu.CompilerParams(vmem_limit_bytes=VMEM_LIMIT)


def on_device(new_pages, routes, resident, queries, own_kv, tables, lengths):
    n_inst, nt = lax.axis_size("inst"), lax.axis_size("tp")
    half = n_inst // 2
    nb = max(b for b in range(1, half + 1) if half % b == 0 and b * b <= half)
    na = half // nb
    requests, heads, groups, head_dim = queries.shape
    resident_count, page = resident.shape[0], resident.shape[2]
    lay = Layout(groups, requests)
    rows = lay.rows
    me, tp = lax.axis_index("inst"), lax.axis_index("tp")
    core, b_at, a_at = me % 2, me // 2 % nb, me // (2 * nb)

    def shift(x, axis, by):
        if axis == "t":
            return lax.ppermute(x, "tp", [(i, (i + by) % nt) for i in range(nt)])
        pairs = []
        for i in range(n_inst):
            c, b, a = i % 2, i // 2 % nb, i // (2 * nb)
            if axis == "a":
                a = (a + by) % na
            elif axis == "b":
                b = (b + by) % nb
            else:
                c = (c + by) % 2
            pairs.append((i, (a * nb + b) * 2 + c))
        return lax.ppermute(x, "inst", pairs)

    sizes = {"a": na, "b": nb, "t": nt}

    def gather(x, axis):
        return [x] + [shift(x, axis, by) for by in range(1, sizes[axis])]

    pool = resident_count + n_inst * CAP
    whole = lengths // page
    places = lax.broadcasted_iota(jnp.int32, tables.shape, 1)
    names = tables[:, :, None] == lax.broadcasted_iota(jnp.int32, (1, 1, pool), 2)
    full = jnp.sum(jnp.where(names & (places < whole[:, None])[:, :, None], 1, 0), axis=1)
    rest = jnp.where(places == whole[:, None], (lengths % page)[:, None], 0)
    part = jnp.sum(jnp.where(names, rest[:, :, None], 0), axis=1)
    width = n_inst * CAP
    planes = -(-2 * width // LANES)
    meta = jnp.concatenate([full[:, resident_count:], part[:, resident_count:]], axis=1)
    meta = jnp.pad(meta, ((0, 0), (0, planes * LANES - 2 * width))).astype(jnp.bfloat16)
    meta = meta.reshape(requests, planes, LANES).transpose(1, 0, 2).reshape(planes * requests, LANES)
    meta_local = jnp.concatenate([full[:, :resident_count], part[:, :resident_count]], axis=1)
    meta_local = jnp.pad(meta_local, ((0, 0), (0, LANES - 2 * resident_count))).astype(jnp.bfloat16)

    query_rows = queries.transpose(1, 2, 0, 3).reshape(heads, rows, head_dim)

    orders = ["b" if k % 2 == 0 else "t" for k in range(heads)]
    gathered = []
    for k in range(heads):
        piece = query_rows[k]
        if k == 0:
            piece = jnp.concatenate([piece, meta], axis=0)
        gathered.append(jnp.stack(gather(piece, "a")))
    other_pages = shift(new_pages, "c", 1)
    first = []
    for k in range(heads):
        first.append(jnp.concatenate(gather(gathered[k], orders[k]), axis=0))
    second = []
    for k in range(heads):
        second.append(gather(first[k], "t" if orders[k] == "b" else "b"))
    metas = first[0][:, rows:]

    page_count = new_pages.shape[0]
    same = routes[:, None] == routes[None, :]
    total_pages = routes.shape[0]
    earlier = lax.broadcasted_iota(jnp.int32, (total_pages, total_pages), 1) < lax.broadcasted_iota(
        jnp.int32, (total_pages, total_pages), 0
    )
    rank = jnp.sum(jnp.where(same & earlier, 1, 0), axis=1).astype(jnp.int32)
    mine = jnp.stack([routes, me * CAP + rank])
    mine = lax.dynamic_slice_in_dim(mine, tp * page_count, page_count, axis=1)
    both = jnp.stack([mine, shift(mine, "c", 1)])
    dest_b = (b_at - jnp.arange(nb, dtype=jnp.int32)) % nb
    dest_a = (a_at - jnp.arange(na, dtype=jnp.int32)) % na
    dest = ((dest_a[None, :] * nb + dest_b[:, None]) * 2 + core).reshape(na * nb)
    hit = both[:, 0][:, None, :] == dest[None, :, None]
    order = lax.broadcasted_iota(jnp.int32, hit.shape, 2)
    count = jnp.sum(jnp.where(hit, 1, 0), axis=2)
    index = jnp.stack(
        [jnp.min(jnp.where(hit, order, page_count - 1), axis=2), jnp.max(jnp.where(hit, order, 0), axis=2)], axis=2
    )
    chosen = index[..., None] == lax.broadcasted_iota(jnp.int32, index.shape + (page_count,), 3)
    column = jnp.sum(jnp.where(chosen, both[:, 1][:, None, None, :], 0), axis=3)
    lists = jnp.concatenate([count[..., None], index, column], axis=2).reshape(-1)
    tp_of_slot = (tp - jnp.arange(nt, dtype=jnp.int32)) % nt
    lists = jnp.concatenate([lists, tp_of_slot]).astype(jnp.int32)

    local, local_lse = pl.pallas_call(
        functools.partial(resident_kernel, lay),
        out_shape=(
            jax.ShapeDtypeStruct((heads, rows, head_dim), jnp.float32),
            jax.ShapeDtypeStruct((-(-heads * lay.lse_rows // 8) * 8, LANES), jnp.float32),
        ),
        in_specs=vmem(4),
        out_specs=tuple(vmem(2)),
        scratch_shapes=[pltpu.VMEM((resident_count, rows, page), jnp.float32)],
        compiler_params=params(),
        name="resident",
    )(query_rows, resident, own_kv.transpose(1, 0, 2), meta_local)

    own_split = new_pages.reshape(page_count, nt, heads, page, 2 * head_dim)
    other_split = other_pages.reshape(page_count, nt, heads, page, 2 * head_dim)

    def attend(k):
        way = orders[k]
        n_out = nt if way == "b" else nb
        blocks = na * nb * nt // n_out
        q_blocks = [x[:, :rows] if k == 0 else x for x in second[k]]
        page_spec = pl.BlockSpec(
            (page_count, nt, 1, page, 2 * head_dim), lambda i: (0, 0, k, 0, 0)
        )
        full_spec = lambda x: pl.BlockSpec(x.shape, lambda i: (0,) * x.ndim)
        lse_lines = blocks * lay.lse_rows
        out = jax.ShapeDtypeStruct((lay.parcel(blocks), head_dim), jnp.bfloat16)
        return pl.pallas_call(
            functools.partial(attend_kernel, (na, nb, nt, way, width), lay),
            grid=(1,),
            out_shape=(out,) * n_out,
            in_specs=[pl.BlockSpec(memory_space=pltpu.SMEM)]
            + [full_spec(x) for x in q_blocks]
            + [full_spec(metas), page_spec, page_spec],
            out_specs=(full_spec(out),) * n_out,
            scratch_shapes=[
                pltpu.VMEM((requests, page), jnp.float32),
                pltpu.VMEM((nt, rows, head_dim), jnp.float32),
                pltpu.VMEM((nt, rows, head_dim), jnp.float32),
                pltpu.VMEM((nt, rows, head_dim), jnp.float32),
                pltpu.VMEM((n_out, lse_lines, LANES), jnp.float32),
                pltpu.VMEM((tail_rows(blocks, lay.lse_rows), LANES), jnp.float32),
            ],
            compiler_params=params(),
            name="attend",
        )(lists, *q_blocks, metas, own_split, other_split)

    def merge(parcels, blocks, parts):
        n = len(parcels)
        each = blocks // parts
        out = jax.ShapeDtypeStruct((lay.parcel(each), head_dim), jnp.bfloat16)
        return pl.pallas_call(
            functools.partial(merge_kernel, n, blocks, parts, lay),
            out_shape=(out,) * parts,
            in_specs=vmem(n),
            out_specs=tuple(vmem(parts)),
            scratch_shapes=[
                pltpu.VMEM((n, blocks * lay.lse_rows, LANES), jnp.float32),
                pltpu.VMEM((blocks * lay.lse_rows, LANES), jnp.float32),
                pltpu.VMEM((tail_rows(blocks, lay.lse_rows), LANES), jnp.float32),
                pltpu.VMEM((tail_rows(each, lay.lse_rows), LANES), jnp.float32),
            ],
            compiler_params=params(),
            name="merge",
        )(*parcels)

    def send_back(parcels, axis):
        return [parcels[0]] + [shift(parcels[by], axis, -by) for by in range(1, len(parcels))]

    arrived = []
    for k in range(heads):
        outer, inner = ("t", "b") if orders[k] == "b" else ("b", "t")
        parcels = send_back(attend(k), outer)
        blocks = na * sizes[inner]
        parcels = send_back(merge(parcels, blocks, sizes[inner]), inner)
        arrived += send_back(merge(parcels, na, na), "a")

    result = pl.pallas_call(
        functools.partial(final_kernel, na, heads, lay),
        out_shape=jax.ShapeDtypeStruct((heads, rows, head_dim), queries.dtype),
        in_specs=vmem(len(arrived) + 2),
        out_specs=vmem(1)[0],
        scratch_shapes=[
            pltpu.VMEM((na + 1, lay.lse_rows, LANES), jnp.float32),
            pltpu.VMEM((tail_rows(1, lay.lse_rows), LANES), jnp.float32),
        ],
        compiler_params=params(),
        name="final",
    )(*arrived, local, local_lse)
    return result.reshape(heads, groups, requests, head_dim).transpose(2, 0, 1, 3)


def solution(mesh):
    return jax.shard_map(
        on_device,
        mesh=mesh,
        in_specs=(
            P(("inst", "tp"), None, None, None),
            P("inst"),
            P("inst", "tp", None, None),
            P("inst", "tp", None, None),
            P("inst", "tp", None),
            P("inst", None),
            P("inst"),
        ),
        out_specs=P("inst", "tp", None, None),
        check_vma=False,
    )
```

```python
import functools
import math

import jax
import jax.numpy as jnp
from jax import lax
from jax.experimental import pallas as pl
from jax.experimental.pallas import tpu as pltpu
from jax.sharding import PartitionSpec as P

CAP = 2
Z_WAIT, R_WAIT, A_WAIT, B_WAIT = 2, 3, 3, 2
DIRECT_OUT = (1, 1, 1, 1)
DIRECT_BACK = (1, 1, 1, 1)
LANES = 128
NEG = -1e30
VMEM_LIMIT = 62 * 1024 * 1024


class Layout:
    def __init__(self, heads, groups, requests, head_dim, width):
        self.heads, self.groups, self.requests, self.head_dim = heads, groups, requests, head_dim
        self.per = LANES // requests
        whole = groups - groups % self.per
        runs = [(h, g) for h in range(heads) for g in range(whole)]
        runs += [(h, g) for h in range(heads) for g in range(whole, groups)]
        self.runs = [runs[i : i + self.per] for i in range(0, len(runs), self.per)]
        self.tiles = len(self.runs)
        self.tiles_of = [
            [i for i, tile in enumerate(self.runs) if any(h == head for h, _ in tile)] for head in range(heads)
        ]
        self.width = width
        self.counts = -(-width // self.per)
        self.data = self.tiles * head_dim
        self.count_rows = -(-2 * self.counts // 16) * 16
        self.tail_rows = -(-3 * self.tiles // 16) * 16
        self.query_rows = self.data + self.count_rows
        self.result_rows = self.data + self.tail_rows

    def mine(self, tile, head):
        owners = [h for h, _ in self.runs[tile]]
        if all(h == head for h in owners) and len(owners) == self.per:
            return None
        run = lax.broadcasted_iota(jnp.int32, (1, LANES), 1) // self.requests
        hits = [run == i for i, h in enumerate(owners) if h == head]
        return functools.reduce(jnp.logical_or, hits)


def rows_of(start, count):
    return pl.ds(start if isinstance(start, int) else pl.multiple_of(start, 16), count)


def store_tail(out, start, lse, tail):
    count = lse.shape[0]
    tail[...] = jnp.zeros_like(tail)
    high = lse.astype(jnp.bfloat16).astype(jnp.float32)
    middle = (lse - high).astype(jnp.bfloat16).astype(jnp.float32)
    tail[0:count] = high
    tail[count : 2 * count] = middle
    tail[2 * count : 3 * count] = lse - high - middle
    out[rows_of(start, tail.shape[0])] = tail[...].astype(jnp.bfloat16)


def load_tail(ref, start, count, tail):
    tail[...] = ref[rows_of(start, tail.shape[0])].astype(jnp.float32)
    return tail[0:count] + tail[count : 2 * count] + tail[2 * count : 3 * count]


def weighted(times):
    return jnp.where(times > 0, jnp.log2(jnp.maximum(times, 1.0)), NEG)


def attend_tiles(lay, count, query_tile, keys, values, bias, scores, extra=None):
    unit = math.log2(math.e) * lay.head_dim ** (-0.5)
    shared = {}
    for j in range(count):
        for head in range(lay.heads):
            mine = lay.tiles_of[head]
            got = jnp.dot(
                keys(j, head),
                jnp.concatenate([query_tile(i) for i in mine], axis=1),
                preferred_element_type=jnp.float32,
            )
            for n, i in enumerate(mine):
                part = got[:, n * LANES : (n + 1) * LANES]
                mask = lay.mine(i, head)
                if mask is None:
                    scores[j, i] = part * unit + bias(j)
                elif (j, i) in shared:
                    shared[j, i] = jnp.where(mask, part, shared[j, i])
                else:
                    shared[j, i] = part
        for i in range(lay.tiles):
            if (j, i) in shared:
                scores[j, i] = shared.pop((j, i)) * unit + bias(j)
    weights, totals, highests = {}, [], []
    for i in range(lay.tiles):
        highest = functools.reduce(jnp.maximum, [scores[j, i] for j in range(count)])
        highest = jnp.max(highest, axis=0, keepdims=True)
        if extra is not None:
            highest = jnp.maximum(highest, extra[i])
        total = None
        for j in range(count):
            value = jnp.exp2(scores[j, i] - highest)
            total = value if total is None else total + value
            weights[j, i] = value.astype(jnp.bfloat16)
        totals.append(jnp.sum(total, axis=0, keepdims=True))
        highests.append(highest)
    mixed = [None] * lay.tiles
    for head in range(lay.heads):
        mine = lay.tiles_of[head]
        got = None
        for j in range(count):
            term = lax.dot_general(
                values(j, head),
                jnp.concatenate([weights[j, i] for i in mine], axis=1),
                (((0,), (0,)), ((), ())),
                preferred_element_type=jnp.float32,
            )
            got = term if got is None else got + term
        for n, i in enumerate(mine):
            part = got[:, n * LANES : (n + 1) * LANES]
            mask = lay.mine(i, head)
            mixed[i] = part if mask is None or mixed[i] is None else jnp.where(mask, part, mixed[i])
    return mixed, totals, highests


def prepare_kernel(lay, first_page, page, q_ref, tables, lengths, out, local, wide, table, line):
    per, requests, dim = lay.per, lay.requests, lay.head_dim
    wide[...] = q_ref[...].astype(jnp.float32)
    for i, runs in enumerate(lay.runs):
        parts = [wide[:, g, h, :] for h, g in runs]
        parts += [jnp.zeros((requests, dim), jnp.float32)] * (per - len(runs))
        out[i * dim : (i + 1) * dim] = jnp.concatenate(parts, axis=0).T.astype(jnp.bfloat16)

    def repeat(ref, value):
        ref[...] = jnp.zeros_like(ref)
        ref[:, 0:requests] = value
        value = ref[...]
        step = requests
        while step < LANES:
            value = value + pltpu.roll(value, step, 1)
            step *= 2
        return value

    slots = tables.shape[0]
    turned, length = repeat(table, tables[...]), repeat(line, lengths[...])
    whole, rest = length // page, length % page

    def count(names):
        full = jnp.zeros(names.shape, jnp.float32)
        part = jnp.zeros(names.shape, jnp.float32)
        for m in range(slots):
            named = turned[m : m + 1] == names
            full = full + jnp.where(named & (whole > m), 1.0, 0.0)
            part = part + jnp.where(named & (whole == m), rest, 0).astype(jnp.float32)
        return full, part

    shape = (lay.count_rows // 2, LANES)
    row = lax.broadcasted_iota(jnp.int32, shape, 0)
    run = lax.broadcasted_iota(jnp.int32, shape, 1) // requests
    full, part = count(first_page + row * per + run)
    out[lay.data :] = jnp.concatenate([full, part], axis=0).astype(jnp.bfloat16)
    shape = (local.shape[0] // 2, LANES)
    full, part = count(lax.broadcasted_iota(jnp.int32, shape, 0))
    local[...] = jnp.concatenate([full, part], axis=0)


def attend_kernel(lay, nb, nt, query_at, result_at, lists, *refs):
    n_in, n_out = (1 + max(which for which, _ in at.values()) for at in (query_at, result_at))
    q_refs, refs = refs[:n_in], refs[n_in:]
    own_pages, other_pages = refs[:2]
    outs, refs = refs[2 : 2 + n_out], refs[2 + n_out :]
    query, result, held, q_sems, out_sems, sems, scores, bias, tail = refs
    most = 2 * CAP
    dim = lay.head_dim
    dests = nb
    heads_at = 5 * 2 * dests
    every = list(query_at)

    def query_copy(sb, st):
        which, block = query_at[sb, st]
        source = q_refs[which].at[pl.ds(block * lay.query_rows, lay.query_rows)]
        return pltpu.make_async_copy(source, query.at[sb, st], q_sems.at[sb, st])

    def result_copy(sb, st):
        which, block = result_at[sb, st]
        goal = outs[which].at[pl.ds(block * lay.result_rows, lay.result_rows)]
        return pltpu.make_async_copy(result.at[sb, st], goal, out_sems.at[sb, st])

    def page_copy(dest, source, j):
        base = (source * dests + dest) * 5
        index = lists[base + 1 + j]
        goal = j if source == 0 else lists[dest * 5] + j
        pages = (own_pages, other_pages)[source]
        return pltpu.make_async_copy(pages.at[index], held.at[dest, goal], sems.at[dest, source, j])

    def each_page(dest, what):
        for source in range(2):
            for j in range(CAP):

                @pl.when(j < lists[(source * dests + dest) * 5])
                def _(source=source, j=j):
                    what(page_copy(dest, source, j))

    def start_pages(dest, carry):
        each_page(dest, lambda copy: copy.start())
        return carry

    for at in every:
        query_copy(*at).start()
    lax.fori_loop(0, dests, start_pages, 0)
    for at in every:
        query_copy(*at).wait()

    position = lax.broadcasted_iota(jnp.int32, (held.shape[-2], LANES), 0).astype(jnp.float32)
    run = lax.broadcasted_iota(jnp.int32, (lay.count_rows, LANES), 1) // lay.requests
    row = lax.broadcasted_iota(jnp.int32, (lay.count_rows, LANES), 0)

    def spread(counts, column, kind):
        here = (row == kind * (lay.count_rows // 2) + column // lay.per) & (run == column % lay.per)
        line = jnp.sum(jnp.where(here, counts, 0.0), axis=0, keepdims=True)
        step = lay.requests
        while step < LANES:
            line = line + pltpu.roll(line, step, 1)
            step *= 2
        return line

    def one_dest(dest, carry):
        count_own, count_other = lists[dest * 5], lists[(dests + dest) * 5]
        count = count_own + count_other
        each_page(dest, lambda copy: copy.wait())

        @pl.when(count == 0)
        def _():
            for st in range(nt):
                result[dest, st, 0 : lay.data] = jnp.zeros((lay.data, LANES), jnp.bfloat16)
                store_tail(
                    result.at[dest, st], lay.data, jnp.full((lay.tiles, LANES), NEG, jnp.float32), tail
                )

        for n in range(1, most + 1):

            @pl.when(count == n)
            def _(n=n):
                counts = query[dest, 0, lay.data :].astype(jnp.float32)
                for j in range(n):
                    from_other = (j >= count_own).astype(jnp.int32)
                    column = lists[(from_other * dests + dest) * 5 + 3 + j - from_other * count_own]
                    full = spread(counts, column, 0)
                    part = spread(counts, column, 1)
                    bias[j] = weighted(full + jnp.where(position < part, 1.0, 0.0))
                for st in range(nt):
                    head_at = lists[heads_at + st]
                    mixed, totals, highests = attend_tiles(
                        lay,
                        n,
                        lambda i: query[dest, st, i * dim : (i + 1) * dim],
                        lambda j, h: held[dest, j, head_at, h, :, :dim],
                        lambda j, h: held[dest, j, head_at, h, :, dim:],
                        lambda j: bias[j],
                        scores.at[st % 2],
                    )
                    lse = []
                    for i in range(lay.tiles):
                        result[dest, st, i * dim : (i + 1) * dim] = (mixed[i] * (1.0 / totals[i])).astype(
                            jnp.bfloat16
                        )
                        lse.append(highests[i] + jnp.log2(totals[i]))
                    store_tail(result.at[dest, st], lay.data, jnp.concatenate(lse, axis=0), tail)

        return carry

    lax.fori_loop(0, dests, one_dest, 0)
    for at in every:
        result_copy(*at).start()
    for at in every:
        result_copy(*at).wait()


def mix(lses):
    highest = functools.reduce(jnp.maximum, lses)
    exps = [jnp.exp2(value - highest) for value in lses]
    total = functools.reduce(jnp.add, exps)
    scale = 1.0 / total
    return [value * scale for value in exps], highest + jnp.log2(total)


def merge_kernel(lay, jobs, *refs):
    ins, refs = refs[: sum(n for n, _ in jobs)], refs[sum(n for n, _ in jobs) :]
    outs, tail = refs[: sum(blocks for _, blocks in jobs)], refs[-1]
    dim = lay.head_dim
    for n, blocks in jobs:
        for b in range(blocks):
            start = b * lay.result_rows
            lses = [load_tail(ref, start + lay.data, lay.tiles, tail) for ref in ins[:n]]
            weights, lse = mix(lses)
            for i in range(lay.tiles):
                terms = [
                    weights[k][i : i + 1] * ins[k][start + i * dim : start + (i + 1) * dim].astype(jnp.float32)
                    for k in range(n)
                ]
                outs[b][i * dim : (i + 1) * dim] = functools.reduce(jnp.add, terms).astype(jnp.bfloat16)
            store_tail(outs[b], lay.data, lse, tail)
        ins, outs = ins[n:], outs[blocks:]


def resident_kernel(lay, q_ref, pages, own, counts, out, lse, scores, wide):
    count, page, dim = pages.shape[0], pages.shape[2], lay.head_dim
    unit = math.log2(math.e) * dim ** (-0.5)
    position = lax.broadcasted_iota(jnp.int32, (page, LANES), 0).astype(jnp.float32)
    offset = counts.shape[0] // 2
    biases = [
        weighted(counts[p : p + 1] + jnp.where(position < counts[offset + p : offset + p + 1], 1.0, 0.0))
        for p in range(count)
    ]

    wide[...] = own[...].astype(jnp.float32)

    def own_tile(i, half):
        parts = [wide[:, h, half * dim : (half + 1) * dim] for h, _ in lay.runs[i]]
        parts += [jnp.zeros((lay.requests, dim), jnp.float32)] * (lay.per - len(parts))
        return jnp.concatenate(parts, axis=0).T

    def query_tile(i):
        return q_ref[i * dim : (i + 1) * dim]

    own_scores = [
        jnp.sum(query_tile(i).astype(jnp.float32) * own_tile(i, 0), axis=0, keepdims=True) * unit
        for i in range(lay.tiles)
    ]
    mixed, totals, highests = attend_tiles(
        lay,
        count,
        query_tile,
        lambda j, h: pages[j, h, :, :dim],
        lambda j, h: pages[j, h, :, dim:],
        lambda j: biases[j],
        scores,
        own_scores,
    )
    lse[...] = jnp.zeros_like(lse)
    for i in range(lay.tiles):
        own_weights = jnp.exp2(own_scores[i] - highests[i])
        total = totals[i] + own_weights
        out[i * dim : (i + 1) * dim] = (mixed[i] + own_weights * own_tile(i, 1)) * (1.0 / total)
        lse[i : i + 1] = highests[i] + jnp.log2(total)


def final_kernel(lay, n, *refs):
    ins, refs = refs[:n], refs[n:]
    local, local_lse, out, tail, wide = refs
    dim, requests = lay.head_dim, lay.requests
    lses = [load_tail(ref, lay.data, lay.tiles, tail) for ref in ins]
    lses.append(local_lse[0 : lay.tiles])
    weights, _ = mix(lses)
    for i, runs in enumerate(lay.runs):
        span = slice(i * dim, (i + 1) * dim)
        total = weights[n][i : i + 1] * local[span]
        for k in range(n):
            total = total + weights[k][i : i + 1] * ins[k][span].astype(jnp.float32)
        turned = total.T
        for r, (h, g) in enumerate(runs):
            wide[:, g, h, :] = turned[r * requests : (r + 1) * requests]
    out[...] = wide[...].astype(out.dtype)


def vmem(count):
    return [pl.BlockSpec(memory_space=pltpu.VMEM)] * count


def params():
    return pltpu.CompilerParams(vmem_limit_bytes=VMEM_LIMIT)


def on_device(new_pages, routes, resident, queries, own_kv, tables, lengths):
    n_inst, nt = lax.axis_size("inst"), lax.axis_size("tp")
    half = n_inst // 2
    nb = max(b for b in range(1, half + 1) if half % b == 0 and b * b <= half)
    na = half // nb
    requests, heads, groups, head_dim = queries.shape
    resident_count, page = resident.shape[0], resident.shape[2]
    width = n_inst * CAP
    lay = Layout(heads, groups, requests, head_dim, width)
    me, tp = lax.axis_index("inst"), lax.axis_index("tp")
    core, b_at, a_at = me % 2, me // 2 % nb, me // (2 * nb)

    def shift(x, axis, by):
        if axis == "t":
            return lax.ppermute(x, "tp", [(i, (i + by) % nt) for i in range(nt)])
        pairs = []
        for i in range(n_inst):
            c, b, a = i % 2, i // 2 % nb, i // (2 * nb)
            if axis == "a":
                a = (a + by) % na
            elif axis == "b":
                b = (b + by) % nb
            else:
                c = (c + by) % 2
            pairs.append((i, (a * nb + b) * 2 + c))
        return lax.ppermute(x, "inst", pairs)

    def shift_both(x, by_b, by_t):
        pairs = []
        for i in range(n_inst):
            b = (i // 2 % nb + by_b) % nb
            goal = (i // (2 * nb) * nb + b) * 2 + i % 2
            pairs += [(i * nt + j, goal * nt + (j + by_t) % nt) for j in range(nt)]
        return lax.ppermute(x, ("inst", "tp"), pairs)

    sizes = {"a": na, "b": nb, "t": nt}
    others = [(sb, st) for sb in range(nb) for st in range(nt)][1:]

    def gather(x, axis):
        return [x] + [shift(x, axis, by) for by in range(1, sizes[axis])]

    local_rows = -(-2 * resident_count // 16) * 16
    block, local_counts = pl.pallas_call(
        functools.partial(prepare_kernel, lay, resident_count, page),
        out_shape=(
            jax.ShapeDtypeStruct((lay.query_rows, LANES), jnp.bfloat16),
            jax.ShapeDtypeStruct((local_rows, LANES), jnp.float32),
        ),
        scratch_shapes=[
            pltpu.VMEM((requests, groups, heads, head_dim), jnp.float32),
            pltpu.VMEM((tables.shape[1], LANES), jnp.int32),
            pltpu.VMEM((1, LANES), jnp.int32),
        ],
        compiler_params=params(),
        name="prepare",
    )(queries.transpose(0, 2, 1, 3), tables.T, lengths[None])

    turns = [0] + sorted(range(1, na), key=lambda s: (min(s, na - s), s))
    small = nb * nt <= 4
    ways, back = {}, {}
    for turn, s in enumerate(turns):
        ways[s] = "bt" if small and DIRECT_OUT[turn] else "bt"[turn % 2]
        back[s] = "bt" if small and DIRECT_BACK[turn] else "bt"[turn % 2]
    other = {"b": "t", "t": "b"}

    def tie(x, *after):
        return lax.optimization_barrier((x, *after))[0]

    other_pages = shift(new_pages, "c", 1)
    def gather_first(x, way):
        if way == "bt":
            return [x] + [shift_both(x, sb, st) for sb, st in others]
        return [jnp.concatenate(gather(x, way), axis=0)]

    def gather_second(got, way):
        return got if way == "bt" else gather(got[0], other[way])

    half_way = {0: gather_first(block, ways[0])}
    direct_first = ways[0] == "bt"
    slots = {}
    for turn, s in enumerate(turns[1:]):
        slots[s] = shift(tie(block, half_way[0][1]) if turn >= Z_WAIT and direct_first else block, "a", s)

    local, local_lse = pl.pallas_call(
        functools.partial(resident_kernel, lay),
        out_shape=(
            jax.ShapeDtypeStruct((lay.data, LANES), jnp.float32),
            jax.ShapeDtypeStruct((-(-lay.tiles // 8) * 8, LANES), jnp.float32),
        ),
        scratch_shapes=[
            pltpu.VMEM((resident_count, lay.tiles, page, LANES), jnp.float32),
            pltpu.VMEM(own_kv.shape, jnp.float32),
        ],
        compiler_params=params(),
        name="resident",
    )(block, resident, own_kv, tie(local_counts, other_pages))

    page_count = new_pages.shape[0]
    same = routes[:, None] == routes[None, :]
    total_pages = routes.shape[0]
    earlier = lax.broadcasted_iota(jnp.int32, (total_pages, total_pages), 1) < lax.broadcasted_iota(
        jnp.int32, (total_pages, total_pages), 0
    )
    rank = jnp.sum(jnp.where(same & earlier, 1, 0), axis=1).astype(jnp.int32)
    mine = jnp.stack([routes, me * CAP + rank])
    mine = lax.dynamic_slice_in_dim(mine, tp * page_count, page_count, axis=1)
    mine = tie(mine, other_pages)
    both = jnp.stack([mine, shift(mine, "c", 1)])
    dest_a = (a_at - jnp.arange(na, dtype=jnp.int32)) % na
    dest_b = (b_at - jnp.arange(nb, dtype=jnp.int32)) % nb
    dest = (dest_a[:, None] * nb + dest_b[None, :]) * 2 + core
    hit = both[None, :, 0, None, :] == dest[:, None, :, None]
    place = lax.broadcasted_iota(jnp.int32, hit.shape, 3)
    count = jnp.sum(jnp.where(hit, 1, 0), axis=3)
    index = jnp.stack(
        [jnp.min(jnp.where(hit, place, page_count - 1), axis=3), jnp.max(jnp.where(hit, place, 0), axis=3)], axis=3
    )
    chosen = index[..., None] == lax.broadcasted_iota(jnp.int32, index.shape + (page_count,), 4)
    column = jnp.sum(jnp.where(chosen, both[None, :, 1, None, None, :], 0), axis=4)
    lists = jnp.concatenate([count[..., None], index, column], axis=3).transpose(1, 0, 2, 3).astype(jnp.int32)
    tp_of_slot = (tp - jnp.arange(nt, dtype=jnp.int32)) % nt

    own_split = new_pages.reshape(page_count, nt, heads, page, 2 * head_dim)
    other_split = other_pages.reshape(page_count, nt, heads, page, 2 * head_dim)

    def places(way):
        every = [(sb, st) for sb in range(nb) for st in range(nt)]
        if way == "bt":
            return {(sb, st): (sb * nt + st, 0) for sb, st in every}
        return {(sb, st): (st, sb) if way == "b" else (sb, st) for sb, st in every}

    def attend(s):
        query_at, result_at = places(ways[s]), places(back[s])
        counts = [0] * (1 + max(which for which, _ in result_at.values()))
        for which, _ in result_at.values():
            counts[which] += 1
        return list(
            pl.pallas_call(
                functools.partial(attend_kernel, lay, nb, nt, query_at, result_at),
                out_shape=tuple(
                    jax.ShapeDtypeStruct((count * lay.result_rows, LANES), jnp.bfloat16) for count in counts
                ),
                in_specs=[pl.BlockSpec(memory_space=pltpu.SMEM)]
                + [pl.BlockSpec(memory_space=pl.ANY)] * (len(gathered[s]) + 2),
                out_specs=(pl.BlockSpec(memory_space=pl.ANY),) * len(counts),
                scratch_shapes=[
                    pltpu.VMEM((nb, nt, lay.query_rows, LANES), jnp.bfloat16),
                    pltpu.VMEM((nb, nt, lay.result_rows, LANES), jnp.bfloat16),
                    pltpu.VMEM((nb, 2 * CAP, nt, heads, page, 2 * head_dim), jnp.bfloat16),
                    pltpu.SemaphoreType.DMA((nb, nt)),
                    pltpu.SemaphoreType.DMA((nb, nt)),
                    pltpu.SemaphoreType.DMA((nb, 2, CAP)),
                    pltpu.VMEM((2, 2 * CAP, lay.tiles, page, LANES), jnp.float32),
                    pltpu.VMEM((2 * CAP, page, LANES), jnp.float32),
                    pltpu.VMEM((lay.tail_rows, LANES), jnp.float32),
                ],
                compiler_params=params(),
                cost_estimate=pl.CostEstimate(flops=0, bytes_accessed=16 << 20, transcendentals=0),
                name="attend",
            )(jnp.concatenate([lists[:, s].reshape(-1), tp_of_slot]), *gathered[s], own_split, other_split)
        )

    def merge(arrays, blocks):
        out = jax.ShapeDtypeStruct((lay.result_rows, LANES), jnp.bfloat16)
        jobs = [(len(x), count) for x, count in zip(arrays, blocks)]
        got = pl.pallas_call(
            functools.partial(merge_kernel, lay, jobs),
            out_shape=(out,) * sum(blocks),
            scratch_shapes=[pltpu.VMEM((lay.tail_rows, LANES), jnp.float32)],
            compiler_params=params(),
            name="merge",
        )(*[x for each in arrays for x in each])
        parts = []
        for count in blocks:
            parts.append(list(got[:count]))
            got = got[count:]
        return parts

    def send_back(arrays, axis):
        return [arrays[0]] + [shift(arrays[by], axis, -by) for by in range(1, len(arrays))]

    def go_back(s):
        parts, way = first_back[s], back[s]
        if way == "bt":
            return [parts[0]] + [shift_both(parts[sb * nt + st], -sb, -st) for sb, st in others]
        parts = merge([send_back(parts, other[way])], [sizes[way]])[0]
        return send_back(parts, way)

    gathered, first_back, returned = {0: gather_second(half_way[0], ways[0])}, {}, {}
    first_back[0] = attend(0)
    for turn, s in enumerate(turns):
        if turn > 0:
            start = slots[s] if turn < R_WAIT else tie(slots[s], local_lse)
            start = start if turn < A_WAIT else tie(start, first_back[0][0])
            gathered[s] = gather_second(gather_first(start, ways[s]), ways[s])
    returned[0] = go_back(0)
    for turn, s in enumerate(turns):
        if turn > 0:
            gathered[s][0] = tie(gathered[s][0], first_back[turns[turn - 1]][0])
            if turn == B_WAIT:
                gathered[s][0] = tie(gathered[s][0], *returned[0][1:])
            first_back[s] = attend(s)
    arrived = list(returned[0])
    for s in turns[1:]:
        arrived.append(shift(merge([go_back(s)], [1])[0][0], "a", -s))

    return pl.pallas_call(
        functools.partial(final_kernel, lay, len(arrived)),
        out_shape=jax.ShapeDtypeStruct((requests, groups, heads, head_dim), queries.dtype),
        scratch_shapes=[
            pltpu.VMEM((lay.tail_rows, LANES), jnp.float32),
            pltpu.VMEM((requests, groups, heads, head_dim), jnp.float32),
        ],
        compiler_params=params(),
        name="final",
    )(*arrived, local, local_lse).transpose(0, 2, 1, 3)


def solution(mesh):
    return jax.shard_map(
        on_device,
        mesh=mesh,
        in_specs=(
            P(("inst", "tp"), None, None, None),
            P("inst"),
            P("inst", "tp", None, None),
            P("inst", "tp", None, None),
            P("inst", "tp", None),
            P("inst", None),
            P("inst"),
        ),
        out_specs=P("inst", "tp", None, None),
        check_vma=False,
    )
```

```python
import functools
import math

import jax
import jax.numpy as jnp
from jax import lax
from jax.experimental import pallas as pl
from jax.experimental.pallas import tpu as pltpu
from jax.sharding import PartitionSpec as P

CAP = 2
Z_WAIT, R_WAIT, A_WAIT, B_WAIT = 2, 3, 3, 2
LANES = 128
NEG = -1e30
VMEM_LIMIT = 64 * 1024 * 1024 - 512 * 1024


class Layout:
    def __init__(self, heads, groups, requests, head_dim, width):
        self.heads, self.groups, self.requests, self.head_dim = heads, groups, requests, head_dim
        self.per = LANES // requests
        whole = groups - groups % self.per
        runs = [(h, g) for h in range(heads) for g in range(whole)]
        runs += [(h, g) for h in range(heads) for g in range(whole, groups)]
        self.runs = [runs[i : i + self.per] for i in range(0, len(runs), self.per)]
        self.tiles = len(self.runs)
        self.tiles_of = [
            [i for i, tile in enumerate(self.runs) if any(h == head for h, _ in tile)] for head in range(heads)
        ]
        self.width = width
        self.counts = -(-width // self.per)
        self.data = self.tiles * head_dim
        self.count_rows = -(-2 * self.counts // 16) * 16
        self.tail_rows = -(-3 * self.tiles // 16) * 16
        self.query_rows = self.data + self.count_rows
        self.result_rows = self.data + self.tail_rows

    def mine(self, tile, head):
        owners = [h for h, _ in self.runs[tile]]
        if all(h == head for h in owners) and len(owners) == self.per:
            return None
        run = lax.broadcasted_iota(jnp.int32, (1, LANES), 1) // self.requests
        hits = [run == i for i, h in enumerate(owners) if h == head]
        return functools.reduce(jnp.logical_or, hits)


def rows_of(start, count):
    return pl.ds(start if isinstance(start, int) else pl.multiple_of(start, 16), count)


def store_tail(out, start, lse, tail):
    count = lse.shape[0]
    tail[...] = jnp.zeros_like(tail)
    high = lse.astype(jnp.bfloat16).astype(jnp.float32)
    middle = (lse - high).astype(jnp.bfloat16).astype(jnp.float32)
    tail[0:count] = high
    tail[count : 2 * count] = middle
    tail[2 * count : 3 * count] = lse - high - middle
    out[rows_of(start, tail.shape[0])] = tail[...].astype(jnp.bfloat16)


def load_tail(ref, start, count, tail):
    tail[...] = ref[rows_of(start, tail.shape[0])].astype(jnp.float32)
    return tail[0:count] + tail[count : 2 * count] + tail[2 * count : 3 * count]


def weighted(times):
    return jnp.where(times > 0, jnp.log2(jnp.maximum(times, 1.0)), NEG)


def attend_tiles(lay, count, query_tile, keys, values, bias, scores, extra=None):
    unit = math.log2(math.e) * lay.head_dim ** (-0.5)
    shared = {}
    for j in range(count):
        for head in range(lay.heads):
            mine = lay.tiles_of[head]
            got = jnp.dot(
                keys(j, head),
                jnp.concatenate([query_tile(i) for i in mine], axis=1),
                preferred_element_type=jnp.float32,
            )
            for n, i in enumerate(mine):
                part = got[:, n * LANES : (n + 1) * LANES]
                mask = lay.mine(i, head)
                if mask is None:
                    scores[j, i] = part * unit + bias(j)
                elif (j, i) in shared:
                    shared[j, i] = jnp.where(mask, part, shared[j, i])
                else:
                    shared[j, i] = part
        for i in range(lay.tiles):
            if (j, i) in shared:
                scores[j, i] = shared.pop((j, i)) * unit + bias(j)
    weights, totals, highests = {}, [], []
    for i in range(lay.tiles):
        highest = functools.reduce(jnp.maximum, [scores[j, i] for j in range(count)])
        highest = jnp.max(highest, axis=0, keepdims=True)
        if extra is not None:
            highest = jnp.maximum(highest, extra[i])
        total = None
        for j in range(count):
            value = jnp.exp2(scores[j, i] - highest)
            total = value if total is None else total + value
            weights[j, i] = value.astype(jnp.bfloat16)
        totals.append(jnp.sum(total, axis=0, keepdims=True))
        highests.append(highest)
    mixed = [None] * lay.tiles
    for head in range(lay.heads):
        mine = lay.tiles_of[head]
        got = None
        for j in range(count):
            term = lax.dot_general(
                values(j, head),
                jnp.concatenate([weights[j, i] for i in mine], axis=1),
                (((0,), (0,)), ((), ())),
                preferred_element_type=jnp.float32,
            )
            got = term if got is None else got + term
        for n, i in enumerate(mine):
            part = got[:, n * LANES : (n + 1) * LANES]
            mask = lay.mine(i, head)
            mixed[i] = part if mask is None or mixed[i] is None else jnp.where(mask, part, mixed[i])
    return mixed, totals, highests


def prepare_kernel(lay, first_page, page, q_ref, tables, lengths, out, local, wide, table, line):
    per, requests, dim = lay.per, lay.requests, lay.head_dim
    wide[...] = q_ref[...].astype(jnp.float32)
    for i, runs in enumerate(lay.runs):
        parts = [wide[:, g, h, :] for h, g in runs]
        parts += [jnp.zeros((requests, dim), jnp.float32)] * (per - len(runs))
        out[i * dim : (i + 1) * dim] = jnp.concatenate(parts, axis=0).T.astype(jnp.bfloat16)

    def repeat(ref, value):
        ref[...] = jnp.zeros_like(ref)
        ref[:, 0:requests] = value
        value = ref[...]
        step = requests
        while step < LANES:
            value = value + pltpu.roll(value, step, 1)
            step *= 2
        return value

    slots = tables.shape[0]
    turned, length = repeat(table, tables[...]), repeat(line, lengths[...])
    whole, rest = length // page, length % page

    def count(names):
        full = jnp.zeros(names.shape, jnp.float32)
        part = jnp.zeros(names.shape, jnp.float32)
        for m in range(slots):
            named = turned[m : m + 1] == names
            full = full + jnp.where(named & (whole > m), 1.0, 0.0)
            part = part + jnp.where(named & (whole == m), rest, 0).astype(jnp.float32)
        return full, part

    shape = (lay.count_rows // 2, LANES)
    row = lax.broadcasted_iota(jnp.int32, shape, 0)
    run = lax.broadcasted_iota(jnp.int32, shape, 1) // requests
    full, part = count(first_page + row * per + run)
    out[lay.data :] = jnp.concatenate([full, part], axis=0).astype(jnp.bfloat16)
    shape = (local.shape[0] // 2, LANES)
    full, part = count(lax.broadcasted_iota(jnp.int32, shape, 0))
    local[...] = jnp.concatenate([full, part], axis=0)


def attend_kernel(lay, nb, nt, query_at, result_at, lists, *refs):
    n_in, n_out = (1 + max(which for which, _ in at.values()) for at in (query_at, result_at))
    q_refs, refs = refs[:n_in], refs[n_in:]
    own_pages, other_pages = refs[:2]
    outs, refs = refs[2 : 2 + n_out], refs[2 + n_out :]
    query, result, held, q_sems, out_sems, sems, scores, bias, tail = refs
    most = 2 * CAP
    dim = lay.head_dim
    dests = nb
    heads_at = 5 * 2 * dests
    every = list(query_at)

    def query_copy(sb, st):
        which, block = query_at[sb, st]
        source = q_refs[which].at[pl.ds(block * lay.query_rows, lay.query_rows)]
        return pltpu.make_async_copy(source, query.at[sb, st], q_sems.at[sb, st])

    def result_copy(sb, st):
        which, block = result_at[sb, st]
        goal = outs[which].at[pl.ds(block * lay.result_rows, lay.result_rows)]
        return pltpu.make_async_copy(result.at[sb, st], goal, out_sems.at[sb, st])

    def page_copy(dest, source, j):
        base = (source * dests + dest) * 5
        index = lists[base + 1 + j]
        goal = j if source == 0 else lists[dest * 5] + j
        pages = (own_pages, other_pages)[source]
        return pltpu.make_async_copy(pages.at[index], held.at[dest, goal], sems.at[dest, source, j])

    def each_page(dest, what):
        for source in range(2):
            for j in range(CAP):

                @pl.when(j < lists[(source * dests + dest) * 5])
                def _(source=source, j=j):
                    what(page_copy(dest, source, j))

    def start_pages(dest, carry):
        each_page(dest, lambda copy: copy.start())
        return carry

    for at in every:
        query_copy(*at).start()
    lax.fori_loop(0, dests, start_pages, 0)
    for at in every:
        query_copy(*at).wait()

    position = lax.broadcasted_iota(jnp.int32, (held.shape[-2], LANES), 0).astype(jnp.float32)
    run = lax.broadcasted_iota(jnp.int32, (lay.count_rows, LANES), 1) // lay.requests
    row = lax.broadcasted_iota(jnp.int32, (lay.count_rows, LANES), 0)

    def spread(counts, column, kind):
        here = (row == kind * (lay.count_rows // 2) + column // lay.per) & (run == column % lay.per)
        line = jnp.sum(jnp.where(here, counts, 0.0), axis=0, keepdims=True)
        step = lay.requests
        while step < LANES:
            line = line + pltpu.roll(line, step, 1)
            step *= 2
        return line

    def one_dest(dest, carry):
        count_own, count_other = lists[dest * 5], lists[(dests + dest) * 5]
        count = count_own + count_other
        each_page(dest, lambda copy: copy.wait())

        @pl.when(count == 0)
        def _():
            for st in range(nt):
                result[dest, st, 0 : lay.data] = jnp.zeros((lay.data, LANES), jnp.bfloat16)
                store_tail(
                    result.at[dest, st], lay.data, jnp.full((lay.tiles, LANES), NEG, jnp.float32), tail
                )

        for n in range(1, most + 1):

            @pl.when(count == n)
            def _(n=n):
                counts = query[dest, 0, lay.data :].astype(jnp.float32)
                for j in range(n):
                    from_other = (j >= count_own).astype(jnp.int32)
                    column = lists[(from_other * dests + dest) * 5 + 3 + j - from_other * count_own]
                    full = spread(counts, column, 0)
                    part = spread(counts, column, 1)
                    bias[j] = weighted(full + jnp.where(position < part, 1.0, 0.0))
                for st in range(nt):
                    head_at = lists[heads_at + st]
                    mixed, totals, highests = attend_tiles(
                        lay,
                        n,
                        lambda i: query[dest, st, i * dim : (i + 1) * dim],
                        lambda j, h: held[dest, j, head_at, h, :, :dim],
                        lambda j, h: held[dest, j, head_at, h, :, dim:],
                        lambda j: bias[j],
                        scores.at[st % 2],
                    )
                    lse = []
                    for i in range(lay.tiles):
                        result[dest, st, i * dim : (i + 1) * dim] = (mixed[i] * (1.0 / totals[i])).astype(
                            jnp.bfloat16
                        )
                        lse.append(highests[i] + jnp.log2(totals[i]))
                    store_tail(result.at[dest, st], lay.data, jnp.concatenate(lse, axis=0), tail)

        return carry

    lax.fori_loop(0, dests, one_dest, 0)
    for at in every:
        result_copy(*at).start()
    for at in every:
        result_copy(*at).wait()


def mix(lses):
    highest = functools.reduce(jnp.maximum, lses)
    exps = [jnp.exp2(value - highest) for value in lses]
    total = functools.reduce(jnp.add, exps)
    scale = 1.0 / total
    return [value * scale for value in exps], highest + jnp.log2(total)


def merge_kernel(lay, jobs, *refs):
    ins, refs = refs[: sum(n for n, _ in jobs)], refs[sum(n for n, _ in jobs) :]
    outs, tail = refs[: sum(blocks for _, blocks in jobs)], refs[-1]
    dim = lay.head_dim
    for n, blocks in jobs:
        for b in range(blocks):
            start = b * lay.result_rows
            lses = [load_tail(ref, start + lay.data, lay.tiles, tail) for ref in ins[:n]]
            weights, lse = mix(lses)
            for i in range(lay.tiles):
                terms = [
                    weights[k][i : i + 1] * ins[k][start + i * dim : start + (i + 1) * dim].astype(jnp.float32)
                    for k in range(n)
                ]
                outs[b][i * dim : (i + 1) * dim] = functools.reduce(jnp.add, terms).astype(jnp.bfloat16)
            store_tail(outs[b], lay.data, lse, tail)
        ins, outs = ins[n:], outs[blocks:]


def resident_kernel(lay, q_ref, pages, own, counts, out, lse, scores, wide):
    count, page, dim = pages.shape[0], pages.shape[2], lay.head_dim
    unit = math.log2(math.e) * dim ** (-0.5)
    position = lax.broadcasted_iota(jnp.int32, (page, LANES), 0).astype(jnp.float32)
    offset = counts.shape[0] // 2
    biases = [
        weighted(counts[p : p + 1] + jnp.where(position < counts[offset + p : offset + p + 1], 1.0, 0.0))
        for p in range(count)
    ]

    wide[...] = own[...].astype(jnp.float32)

    def own_tile(i, half):
        parts = [wide[:, h, half * dim : (half + 1) * dim] for h, _ in lay.runs[i]]
        parts += [jnp.zeros((lay.requests, dim), jnp.float32)] * (lay.per - len(parts))
        return jnp.concatenate(parts, axis=0).T

    def query_tile(i):
        return q_ref[i * dim : (i + 1) * dim]

    own_scores = [
        jnp.sum(query_tile(i).astype(jnp.float32) * own_tile(i, 0), axis=0, keepdims=True) * unit
        for i in range(lay.tiles)
    ]
    mixed, totals, highests = attend_tiles(
        lay,
        count,
        query_tile,
        lambda j, h: pages[j, h, :, :dim],
        lambda j, h: pages[j, h, :, dim:],
        lambda j: biases[j],
        scores,
        own_scores,
    )
    lse[...] = jnp.zeros_like(lse)
    for i in range(lay.tiles):
        own_weights = jnp.exp2(own_scores[i] - highests[i])
        total = totals[i] + own_weights
        out[i * dim : (i + 1) * dim] = (mixed[i] + own_weights * own_tile(i, 1)) * (1.0 / total)
        lse[i : i + 1] = highests[i] + jnp.log2(total)


def final_kernel(lay, n, *refs):
    ins, refs = refs[:n], refs[n:]
    local, local_lse, out, tail, wide = refs
    dim, requests = lay.head_dim, lay.requests
    lses = [load_tail(ref, lay.data, lay.tiles, tail) for ref in ins]
    lses.append(local_lse[0 : lay.tiles])
    weights, _ = mix(lses)
    for i, runs in enumerate(lay.runs):
        span = slice(i * dim, (i + 1) * dim)
        total = weights[n][i : i + 1] * local[span]
        for k in range(n):
            total = total + weights[k][i : i + 1] * ins[k][span].astype(jnp.float32)
        turned = total.T
        for r, (h, g) in enumerate(runs):
            wide[:, g, h, :] = turned[r * requests : (r + 1) * requests]
    out[...] = wide[...].astype(out.dtype)


def vmem(count):
    return [pl.BlockSpec(memory_space=pltpu.VMEM)] * count


def params():
    return pltpu.CompilerParams(vmem_limit_bytes=VMEM_LIMIT)


def on_device(new_pages, routes, resident, queries, own_kv, tables, lengths):
    n_inst, nt = lax.axis_size("inst"), lax.axis_size("tp")
    half = n_inst // 2
    nb = max(b for b in range(1, half + 1) if half % b == 0 and b * b <= half)
    na = half // nb
    requests, heads, groups, head_dim = queries.shape
    resident_count, page = resident.shape[0], resident.shape[2]
    width = n_inst * CAP
    lay = Layout(heads, groups, requests, head_dim, width)
    me, tp = lax.axis_index("inst"), lax.axis_index("tp")
    core, b_at, a_at = me % 2, me // 2 % nb, me // (2 * nb)

    def shift(x, axis, by):
        if axis == "t":
            return lax.ppermute(x, "tp", [(i, (i + by) % nt) for i in range(nt)])
        pairs = []
        for i in range(n_inst):
            c, b, a = i % 2, i // 2 % nb, i // (2 * nb)
            if axis == "a":
                a = (a + by) % na
            elif axis == "b":
                b = (b + by) % nb
            else:
                c = (c + by) % 2
            pairs.append((i, (a * nb + b) * 2 + c))
        return lax.ppermute(x, "inst", pairs)

    def shift_both(x, by_b, by_t):
        pairs = []
        for i in range(n_inst):
            b = (i // 2 % nb + by_b) % nb
            goal = (i // (2 * nb) * nb + b) * 2 + i % 2
            pairs += [(i * nt + j, goal * nt + (j + by_t) % nt) for j in range(nt)]
        return lax.ppermute(x, ("inst", "tp"), pairs)

    sizes = {"a": na, "b": nb, "t": nt}
    others = [(sb, st) for sb in range(nb) for st in range(nt)][1:]

    def gather(x, axis):
        return [x] + [shift(x, axis, by) for by in range(1, sizes[axis])]

    local_rows = -(-2 * resident_count // 16) * 16
    block, local_counts = pl.pallas_call(
        functools.partial(prepare_kernel, lay, resident_count, page),
        out_shape=(
            jax.ShapeDtypeStruct((lay.query_rows, LANES), jnp.bfloat16),
            jax.ShapeDtypeStruct((local_rows, LANES), jnp.float32),
        ),
        scratch_shapes=[
            pltpu.VMEM((requests, groups, heads, head_dim), jnp.float32),
            pltpu.VMEM((tables.shape[1], LANES), jnp.int32),
            pltpu.VMEM((1, LANES), jnp.int32),
        ],
        compiler_params=params(),
        name="prepare",
    )(queries.transpose(0, 2, 1, 3), tables.T, lengths[None])

    turns = [0, *range(1, na)]
    small = nb * nt <= 4
    ways, back = {}, {}
    for turn, s in enumerate(turns):
        ways[s] = back[s] = "bt" if small else "bt"[turn % 2]
    other = {"b": "t", "t": "b"}

    def tie(x, *after):
        return lax.optimization_barrier((x, *after))[0]

    other_pages = shift(new_pages, "c", 1)
    def gather_first(x, way):
        if way == "bt":
            return [x] + [shift_both(x, sb, st) for sb, st in others]
        return [jnp.concatenate(gather(x, way), axis=0)]

    def gather_second(got, way):
        return got if way == "bt" else gather(got[0], other[way])

    half_way = {0: gather_first(block, ways[0])}
    direct_first = ways[0] == "bt"
    slots = {}
    for turn, s in enumerate(turns[1:]):
        slots[s] = shift(tie(block, half_way[0][1]) if turn >= Z_WAIT and direct_first else block, "a", s)

    local, local_lse = pl.pallas_call(
        functools.partial(resident_kernel, lay),
        out_shape=(
            jax.ShapeDtypeStruct((lay.data, LANES), jnp.float32),
            jax.ShapeDtypeStruct((-(-lay.tiles // 8) * 8, LANES), jnp.float32),
        ),
        scratch_shapes=[
            pltpu.VMEM((resident_count, lay.tiles, page, LANES), jnp.float32),
            pltpu.VMEM(own_kv.shape, jnp.float32),
        ],
        compiler_params=params(),
        name="resident",
    )(block, resident, own_kv, tie(local_counts, other_pages))

    page_count = new_pages.shape[0]
    same = routes[:, None] == routes[None, :]
    total_pages = routes.shape[0]
    earlier = lax.broadcasted_iota(jnp.int32, (total_pages, total_pages), 1) < lax.broadcasted_iota(
        jnp.int32, (total_pages, total_pages), 0
    )
    rank = jnp.sum(jnp.where(same & earlier, 1, 0), axis=1).astype(jnp.int32)
    mine = jnp.stack([routes, me * CAP + rank])
    mine = lax.dynamic_slice_in_dim(mine, tp * page_count, page_count, axis=1)
    mine = tie(mine, other_pages)
    both = jnp.stack([mine, shift(mine, "c", 1)])
    dest_a = (a_at - jnp.arange(na, dtype=jnp.int32)) % na
    dest_b = (b_at - jnp.arange(nb, dtype=jnp.int32)) % nb
    dest = (dest_a[:, None] * nb + dest_b[None, :]) * 2 + core
    hit = both[None, :, 0, None, :] == dest[:, None, :, None]
    place = lax.broadcasted_iota(jnp.int32, hit.shape, 3)
    count = jnp.sum(jnp.where(hit, 1, 0), axis=3)
    index = jnp.stack(
        [jnp.min(jnp.where(hit, place, page_count - 1), axis=3), jnp.max(jnp.where(hit, place, 0), axis=3)], axis=3
    )
    chosen = index[..., None] == lax.broadcasted_iota(jnp.int32, index.shape + (page_count,), 4)
    column = jnp.sum(jnp.where(chosen, both[None, :, 1, None, None, :], 0), axis=4)
    lists = jnp.concatenate([count[..., None], index, column], axis=3).transpose(1, 0, 2, 3).astype(jnp.int32)
    tp_of_slot = (tp - jnp.arange(nt, dtype=jnp.int32)) % nt

    own_split = new_pages.reshape(page_count, nt, heads, page, 2 * head_dim)
    other_split = other_pages.reshape(page_count, nt, heads, page, 2 * head_dim)

    def places(way):
        every = [(sb, st) for sb in range(nb) for st in range(nt)]
        if way == "bt":
            return {(sb, st): (sb * nt + st, 0) for sb, st in every}
        return {(sb, st): (st, sb) if way == "b" else (sb, st) for sb, st in every}

    def attend(s):
        query_at, result_at = places(ways[s]), places(back[s])
        counts = [0] * (1 + max(which for which, _ in result_at.values()))
        for which, _ in result_at.values():
            counts[which] += 1
        return list(
            pl.pallas_call(
                functools.partial(attend_kernel, lay, nb, nt, query_at, result_at),
                out_shape=tuple(
                    jax.ShapeDtypeStruct((count * lay.result_rows, LANES), jnp.bfloat16) for count in counts
                ),
                in_specs=[pl.BlockSpec(memory_space=pltpu.SMEM)]
                + [pl.BlockSpec(memory_space=pl.ANY)] * (len(gathered[s]) + 2),
                out_specs=(pl.BlockSpec(memory_space=pl.ANY),) * len(counts),
                scratch_shapes=[
                    pltpu.VMEM((nb, nt, lay.query_rows, LANES), jnp.bfloat16),
                    pltpu.VMEM((nb, nt, lay.result_rows, LANES), jnp.bfloat16),
                    pltpu.VMEM((nb, 2 * CAP, nt, heads, page, 2 * head_dim), jnp.bfloat16),
                    pltpu.SemaphoreType.DMA((nb, nt)),
                    pltpu.SemaphoreType.DMA((nb, nt)),
                    pltpu.SemaphoreType.DMA((nb, 2, CAP)),
                    pltpu.VMEM((2, 2 * CAP, lay.tiles, page, LANES), jnp.float32),
                    pltpu.VMEM((2 * CAP, page, LANES), jnp.float32),
                    pltpu.VMEM((lay.tail_rows, LANES), jnp.float32),
                ],
                compiler_params=params(),
                cost_estimate=pl.CostEstimate(flops=0, bytes_accessed=16 << 20, transcendentals=0),
                name="attend",
            )(jnp.concatenate([lists[:, s].reshape(-1), tp_of_slot]), *gathered[s], own_split, other_split)
        )

    def merge(arrays, blocks):
        out = jax.ShapeDtypeStruct((lay.result_rows, LANES), jnp.bfloat16)
        jobs = [(len(x), count) for x, count in zip(arrays, blocks)]
        got = pl.pallas_call(
            functools.partial(merge_kernel, lay, jobs),
            out_shape=(out,) * sum(blocks),
            scratch_shapes=[pltpu.VMEM((lay.tail_rows, LANES), jnp.float32)],
            compiler_params=params(),
            name="merge",
        )(*[x for each in arrays for x in each])
        parts = []
        for count in blocks:
            parts.append(list(got[:count]))
            got = got[count:]
        return parts

    def send_back(arrays, axis):
        return [arrays[0]] + [shift(arrays[by], axis, -by) for by in range(1, len(arrays))]

    def go_back(s):
        parts, way = first_back[s], back[s]
        if way == "bt":
            return [parts[0]] + [shift_both(parts[sb * nt + st], -sb, -st) for sb, st in others]
        parts = merge([send_back(parts, other[way])], [sizes[way]])[0]
        return send_back(parts, way)

    gathered, first_back, returned = {0: gather_second(half_way[0], ways[0])}, {}, {}
    first_back[0] = attend(0)
    for turn, s in enumerate(turns):
        if turn > 0:
            start = slots[s] if turn < R_WAIT else tie(slots[s], local_lse)
            start = start if turn < A_WAIT else tie(start, first_back[0][0])
            gathered[s] = gather_second(gather_first(start, ways[s]), ways[s])
    returned[0] = go_back(0)
    for turn, s in enumerate(turns):
        if turn > 0:
            gathered[s][0] = tie(gathered[s][0], first_back[turns[turn - 1]][0])
            if turn == B_WAIT:
                gathered[s][0] = tie(gathered[s][0], *returned[0][1:])
            first_back[s] = attend(s)
    arrived = list(returned[0])
    for s in turns[1:]:
        arrived.append(shift(merge([go_back(s)], [1])[0][0], "a", -s))

    return pl.pallas_call(
        functools.partial(final_kernel, lay, len(arrived)),
        out_shape=jax.ShapeDtypeStruct((requests, groups, heads, head_dim), queries.dtype),
        scratch_shapes=[
            pltpu.VMEM((lay.tail_rows, LANES), jnp.float32),
            pltpu.VMEM((requests, groups, heads, head_dim), jnp.float32),
        ],
        compiler_params=params(),
        name="final",
    )(*arrived, local, local_lse).transpose(0, 2, 1, 3)


def solution(mesh):
    return jax.shard_map(
        on_device,
        mesh=mesh,
        in_specs=(
            P(("inst", "tp"), None, None, None),
            P("inst"),
            P("inst", "tp", None, None),
            P("inst", "tp", None, None),
            P("inst", "tp", None),
            P("inst", None),
            P("inst"),
        ),
        out_specs=P("inst", "tp", None, None),
        check_vma=False,
    )
```

```python
import functools
import math

import jax
import jax.numpy as jnp
from jax import lax
from jax.experimental import pallas as pl
from jax.experimental.pallas import tpu as pltpu
from jax.sharding import PartitionSpec as P

CAP = 2
Z_WAIT, R_WAIT, A_WAIT, B_WAIT = 2, 3, 3, 2
LANES = 128
NEG = -1e30
VMEM_LIMIT = 64 * 1024 * 1024 - 512 * 1024


class Layout:
    def __init__(self, heads, groups, requests, head_dim, width):
        self.heads, self.groups, self.requests, self.head_dim = heads, groups, requests, head_dim
        self.per = LANES // requests
        whole = groups - groups % self.per
        runs = [(h, g) for h in range(heads) for g in range(whole)]
        runs += [(h, g) for h in range(heads) for g in range(whole, groups)]
        self.runs = [runs[i : i + self.per] for i in range(0, len(runs), self.per)]
        self.tiles = len(self.runs)
        self.tiles_of = [
            [i for i, tile in enumerate(self.runs) if any(h == head for h, _ in tile)] for head in range(heads)
        ]
        self.width = width
        self.counts = -(-width // self.per)
        self.data = self.tiles * head_dim
        self.count_rows = -(-2 * self.counts // 16) * 16
        self.tail_rows = -(-3 * self.tiles // 16) * 16
        self.query_rows = self.data + self.count_rows
        self.result_rows = self.data + self.tail_rows

    def mine(self, tile, head):
        owners = [h for h, _ in self.runs[tile]]
        if all(h == head for h in owners) and len(owners) == self.per:
            return None
        run = lax.broadcasted_iota(jnp.int32, (1, LANES), 1) // self.requests
        hits = [run == i for i, h in enumerate(owners) if h == head]
        return functools.reduce(jnp.logical_or, hits)


def rows_of(start, count):
    return pl.ds(start if isinstance(start, int) else pl.multiple_of(start, 16), count)


def store_tail(out, start, lse, tail):
    count = lse.shape[0]
    tail[...] = jnp.zeros_like(tail)
    high = lse.astype(jnp.bfloat16).astype(jnp.float32)
    middle = (lse - high).astype(jnp.bfloat16).astype(jnp.float32)
    tail[0:count] = high
    tail[count : 2 * count] = middle
    tail[2 * count : 3 * count] = lse - high - middle
    out[rows_of(start, tail.shape[0])] = tail[...].astype(jnp.bfloat16)


def load_tail(ref, start, count, tail):
    tail[...] = ref[rows_of(start, tail.shape[0])].astype(jnp.float32)
    return tail[0:count] + tail[count : 2 * count] + tail[2 * count : 3 * count]


def weighted(times):
    return jnp.where(times > 0, jnp.log2(jnp.maximum(times, 1.0)), NEG)


def attend_tiles(lay, count, query_tile, keys, values, bias, scores, extra=None):
    unit = math.log2(math.e) * lay.head_dim ** (-0.5)
    shared = {}
    for j in range(count):
        for head in range(lay.heads):
            mine = lay.tiles_of[head]
            got = jnp.dot(
                keys(j, head),
                jnp.concatenate([query_tile(i) for i in mine], axis=1),
                preferred_element_type=jnp.float32,
            )
            for n, i in enumerate(mine):
                part = got[:, n * LANES : (n + 1) * LANES]
                mask = lay.mine(i, head)
                if mask is None:
                    scores[j, i] = part * unit + bias(j)
                elif (j, i) in shared:
                    shared[j, i] = jnp.where(mask, part, shared[j, i])
                else:
                    shared[j, i] = part
        for i in range(lay.tiles):
            if (j, i) in shared:
                scores[j, i] = shared.pop((j, i)) * unit + bias(j)
    weights, totals, highests = {}, [], []
    for i in range(lay.tiles):
        highest = functools.reduce(jnp.maximum, [scores[j, i] for j in range(count)])
        highest = jnp.max(highest, axis=0, keepdims=True)
        if extra is not None:
            highest = jnp.maximum(highest, extra[i])
        total = None
        for j in range(count):
            value = jnp.exp2(scores[j, i] - highest)
            total = value if total is None else total + value
            weights[j, i] = value.astype(jnp.bfloat16)
        totals.append(jnp.sum(total, axis=0, keepdims=True))
        highests.append(highest)
    mixed = [None] * lay.tiles
    for head in range(lay.heads):
        mine = lay.tiles_of[head]
        got = None
        for j in range(count):
            term = lax.dot_general(
                values(j, head),
                jnp.concatenate([weights[j, i] for i in mine], axis=1),
                (((0,), (0,)), ((), ())),
                preferred_element_type=jnp.float32,
            )
            got = term if got is None else got + term
        for n, i in enumerate(mine):
            part = got[:, n * LANES : (n + 1) * LANES]
            mask = lay.mine(i, head)
            mixed[i] = part if mask is None or mixed[i] is None else jnp.where(mask, part, mixed[i])
    return mixed, totals, highests


def prepare_kernel(lay, first_page, page, q_ref, tables, lengths, out, local, wide, table, line):
    per, requests, dim = lay.per, lay.requests, lay.head_dim
    wide[...] = q_ref[...].astype(jnp.float32)
    for i, runs in enumerate(lay.runs):
        parts = [wide[:, g, h, :] for h, g in runs]
        parts += [jnp.zeros((requests, dim), jnp.float32)] * (per - len(runs))
        out[i * dim : (i + 1) * dim] = jnp.concatenate(parts, axis=0).T.astype(jnp.bfloat16)

    def repeat(ref, value):
        ref[...] = jnp.zeros_like(ref)
        ref[:, 0:requests] = value
        value = ref[...]
        step = requests
        while step < LANES:
            value = value + pltpu.roll(value, step, 1)
            step *= 2
        return value

    slots = tables.shape[0]
    turned, length = repeat(table, tables[...]), repeat(line, lengths[...])
    whole, rest = length // page, length % page

    def count(names):
        full = jnp.zeros(names.shape, jnp.float32)
        part = jnp.zeros(names.shape, jnp.float32)
        for m in range(slots):
            named = turned[m : m + 1] == names
            full = full + jnp.where(named & (whole > m), 1.0, 0.0)
            part = part + jnp.where(named & (whole == m), rest, 0).astype(jnp.float32)
        return full, part

    shape = (lay.count_rows // 2, LANES)
    row = lax.broadcasted_iota(jnp.int32, shape, 0)
    run = lax.broadcasted_iota(jnp.int32, shape, 1) // requests
    full, part = count(first_page + row * per + run)
    out[lay.data :] = jnp.concatenate([full, part], axis=0).astype(jnp.bfloat16)
    shape = (local.shape[0] // 2, LANES)
    full, part = count(lax.broadcasted_iota(jnp.int32, shape, 0))
    local[...] = jnp.concatenate([full, part], axis=0)


def attend_kernel(lay, nb, nt, query_at, result_at, lists, *refs):
    n_in, n_out = (1 + max(which for which, _ in at.values()) for at in (query_at, result_at))
    q_refs, refs = refs[:n_in], refs[n_in:]
    own_pages, other_pages = refs[:2]
    outs, refs = refs[2 : 2 + n_out], refs[2 + n_out :]
    query, result, held, q_sems, out_sems, sems, scores, bias, tail = refs
    most = 2 * CAP
    dim = lay.head_dim
    dests = nb
    heads_at = 5 * 2 * dests
    every = list(query_at)

    def query_copy(sb, st):
        which, block = query_at[sb, st]
        source = q_refs[which].at[pl.ds(block * lay.query_rows, lay.query_rows)]
        return pltpu.make_async_copy(source, query.at[sb, st], q_sems.at[sb, st])

    def result_copy(sb, st):
        which, block = result_at[sb, st]
        goal = outs[which].at[pl.ds(block * lay.result_rows, lay.result_rows)]
        return pltpu.make_async_copy(result.at[sb, st], goal, out_sems.at[sb, st])

    def page_copy(dest, source, j):
        base = (source * dests + dest) * 5
        index = lists[base + 1 + j]
        goal = j if source == 0 else lists[dest * 5] + j
        pages = (own_pages, other_pages)[source]
        return pltpu.make_async_copy(pages.at[index], held.at[dest, goal], sems.at[dest, source, j])

    def each_page(dest, what):
        for source in range(2):
            for j in range(CAP):

                @pl.when(j < lists[(source * dests + dest) * 5])
                def _(source=source, j=j):
                    what(page_copy(dest, source, j))

    def start_pages(dest, carry):
        each_page(dest, lambda copy: copy.start())
        return carry

    for at in every:
        query_copy(*at).start()
    lax.fori_loop(0, dests, start_pages, 0)
    for at in every:
        query_copy(*at).wait()

    position = lax.broadcasted_iota(jnp.int32, (held.shape[-2], LANES), 0).astype(jnp.float32)
    run = lax.broadcasted_iota(jnp.int32, (lay.count_rows, LANES), 1) // lay.requests
    row = lax.broadcasted_iota(jnp.int32, (lay.count_rows, LANES), 0)

    def spread(counts, column, kind):
        here = (row == kind * (lay.count_rows // 2) + column // lay.per) & (run == column % lay.per)
        line = jnp.sum(jnp.where(here, counts, 0.0), axis=0, keepdims=True)
        step = lay.requests
        while step < LANES:
            line = line + pltpu.roll(line, step, 1)
            step *= 2
        return line

    def one_dest(dest, carry):
        count_own, count_other = lists[dest * 5], lists[(dests + dest) * 5]
        count = count_own + count_other
        each_page(dest, lambda copy: copy.wait())

        @pl.when(count == 0)
        def _():
            for st in range(nt):
                result[dest, st, 0 : lay.data] = jnp.zeros((lay.data, LANES), jnp.bfloat16)
                store_tail(
                    result.at[dest, st], lay.data, jnp.full((lay.tiles, LANES), NEG, jnp.float32), tail
                )

        for n in range(1, most + 1):

            @pl.when(count == n)
            def _(n=n):
                counts = query[dest, 0, lay.data :].astype(jnp.float32)
                for j in range(n):
                    from_other = (j >= count_own).astype(jnp.int32)
                    column = lists[(from_other * dests + dest) * 5 + 3 + j - from_other * count_own]
                    full = spread(counts, column, 0)
                    part = spread(counts, column, 1)
                    bias[j] = weighted(full + jnp.where(position < part, 1.0, 0.0))
                for st in range(nt):
                    head_at = lists[heads_at + st]
                    mixed, totals, highests = attend_tiles(
                        lay,
                        n,
                        lambda i: query[dest, st, i * dim : (i + 1) * dim],
                        lambda j, h: held[dest, j, head_at, h, :, :dim],
                        lambda j, h: held[dest, j, head_at, h, :, dim:],
                        lambda j: bias[j],
                        scores.at[st % 2],
                    )
                    lse = []
                    for i in range(lay.tiles):
                        result[dest, st, i * dim : (i + 1) * dim] = (mixed[i] * (1.0 / totals[i])).astype(
                            jnp.bfloat16
                        )
                        lse.append(highests[i] + jnp.log2(totals[i]))
                    store_tail(result.at[dest, st], lay.data, jnp.concatenate(lse, axis=0), tail)

        return carry

    lax.fori_loop(0, dests, one_dest, 0)
    for at in every:
        result_copy(*at).start()
    for at in every:
        result_copy(*at).wait()


def mix(lses):
    highest = functools.reduce(jnp.maximum, lses)
    exps = [jnp.exp2(value - highest) for value in lses]
    total = functools.reduce(jnp.add, exps)
    scale = 1.0 / total
    return [value * scale for value in exps], highest + jnp.log2(total)


def merge_kernel(lay, jobs, *refs):
    ins, refs = refs[: sum(n for n, _ in jobs)], refs[sum(n for n, _ in jobs) :]
    outs, tail = refs[: sum(blocks for _, blocks in jobs)], refs[-1]
    dim = lay.head_dim
    for n, blocks in jobs:
        for b in range(blocks):
            start = b * lay.result_rows
            lses = [load_tail(ref, start + lay.data, lay.tiles, tail) for ref in ins[:n]]
            weights, lse = mix(lses)
            for i in range(lay.tiles):
                terms = [
                    weights[k][i : i + 1] * ins[k][start + i * dim : start + (i + 1) * dim].astype(jnp.float32)
                    for k in range(n)
                ]
                outs[b][i * dim : (i + 1) * dim] = functools.reduce(jnp.add, terms).astype(jnp.bfloat16)
            store_tail(outs[b], lay.data, lse, tail)
        ins, outs = ins[n:], outs[blocks:]


def resident_kernel(lay, q_ref, pages, own, counts, out, lse, scores, wide):
    count, page, dim = pages.shape[0], pages.shape[2], lay.head_dim
    unit = math.log2(math.e) * dim ** (-0.5)
    position = lax.broadcasted_iota(jnp.int32, (page, LANES), 0).astype(jnp.float32)
    offset = counts.shape[0] // 2
    biases = [
        weighted(counts[p : p + 1] + jnp.where(position < counts[offset + p : offset + p + 1], 1.0, 0.0))
        for p in range(count)
    ]

    wide[...] = own[...].astype(jnp.float32)

    def own_tile(i, half):
        parts = [wide[:, h, half * dim : (half + 1) * dim] for h, _ in lay.runs[i]]
        parts += [jnp.zeros((lay.requests, dim), jnp.float32)] * (lay.per - len(parts))
        return jnp.concatenate(parts, axis=0).T

    def query_tile(i):
        return q_ref[i * dim : (i + 1) * dim]

    own_scores = [
        jnp.sum(query_tile(i).astype(jnp.float32) * own_tile(i, 0), axis=0, keepdims=True) * unit
        for i in range(lay.tiles)
    ]
    mixed, totals, highests = attend_tiles(
        lay,
        count,
        query_tile,
        lambda j, h: pages[j, h, :, :dim],
        lambda j, h: pages[j, h, :, dim:],
        lambda j: biases[j],
        scores,
        own_scores,
    )
    lse[...] = jnp.zeros_like(lse)
    for i in range(lay.tiles):
        own_weights = jnp.exp2(own_scores[i] - highests[i])
        total = totals[i] + own_weights
        out[i * dim : (i + 1) * dim] = (mixed[i] + own_weights * own_tile(i, 1)) * (1.0 / total)
        lse[i : i + 1] = highests[i] + jnp.log2(total)


def final_kernel(lay, n, *refs):
    ins, refs = refs[:n], refs[n:]
    local, local_lse, out, tail, wide = refs
    dim, requests = lay.head_dim, lay.requests
    lses = [load_tail(ref, lay.data, lay.tiles, tail) for ref in ins]
    lses.append(local_lse[0 : lay.tiles])
    weights, _ = mix(lses)
    for i, runs in enumerate(lay.runs):
        span = slice(i * dim, (i + 1) * dim)
        total = weights[n][i : i + 1] * local[span]
        for k in range(n):
            total = total + weights[k][i : i + 1] * ins[k][span].astype(jnp.float32)
        turned = total.T
        for r, (h, g) in enumerate(runs):
            wide[:, g, h, :] = turned[r * requests : (r + 1) * requests]
    out[...] = wide[...].astype(out.dtype)


def vmem(count):
    return [pl.BlockSpec(memory_space=pltpu.VMEM)] * count


def params():
    return pltpu.CompilerParams(vmem_limit_bytes=VMEM_LIMIT)


def on_device(new_pages, routes, resident, queries, own_kv, tables, lengths):
    n_inst, nt = lax.axis_size("inst"), lax.axis_size("tp")
    half = n_inst // 2
    nb = max(b for b in range(1, half + 1) if half % b == 0 and b * b <= half)
    na = half // nb
    requests, heads, groups, head_dim = queries.shape
    resident_count, page = resident.shape[0], resident.shape[2]
    width = n_inst * CAP
    lay = Layout(heads, groups, requests, head_dim, width)
    me, tp = lax.axis_index("inst"), lax.axis_index("tp")
    core, b_at, a_at = me % 2, me // 2 % nb, me // (2 * nb)

    def shift(x, axis, by):
        if axis == "t":
            return lax.ppermute(x, "tp", [(i, (i + by) % nt) for i in range(nt)])
        pairs = []
        for i in range(n_inst):
            c, b, a = i % 2, i // 2 % nb, i // (2 * nb)
            if axis == "a":
                a = (a + by) % na
            elif axis == "b":
                b = (b + by) % nb
            else:
                c = (c + by) % 2
            pairs.append((i, (a * nb + b) * 2 + c))
        return lax.ppermute(x, "inst", pairs)

    def shift_both(x, by_b, by_t):
        pairs = []
        for i in range(n_inst):
            b = (i // 2 % nb + by_b) % nb
            goal = (i // (2 * nb) * nb + b) * 2 + i % 2
            pairs += [(i * nt + j, goal * nt + (j + by_t) % nt) for j in range(nt)]
        return lax.ppermute(x, ("inst", "tp"), pairs)

    sizes = {"a": na, "b": nb, "t": nt}
    others = [(sb, st) for sb in range(nb) for st in range(nt)][1:]

    def gather(x, axis):
        return [x] + [shift(x, axis, by) for by in range(1, sizes[axis])]

    local_rows = -(-2 * resident_count // 16) * 16
    block, local_counts = pl.pallas_call(
        functools.partial(prepare_kernel, lay, resident_count, page),
        out_shape=(
            jax.ShapeDtypeStruct((lay.query_rows, LANES), jnp.bfloat16),
            jax.ShapeDtypeStruct((local_rows, LANES), jnp.float32),
        ),
        scratch_shapes=[
            pltpu.VMEM((requests, groups, heads, head_dim), jnp.float32),
            pltpu.VMEM((tables.shape[1], LANES), jnp.int32),
            pltpu.VMEM((1, LANES), jnp.int32),
        ],
        compiler_params=params(),
        name="prepare",
    )(queries.transpose(0, 2, 1, 3), tables.T, lengths[None])

    turns = [0, *range(1, na)]
    small = nb * nt <= 4
    ways, back = {}, {}
    for turn, s in enumerate(turns):
        ways[s] = back[s] = "bt" if small else "bt"[turn % 2]
    other = {"b": "t", "t": "b"}

    def tie(x, *after):
        return lax.optimization_barrier((x, *after))[0]

    other_pages = shift(new_pages, "c", 1)
    def gather_first(x, way):
        if way == "bt":
            return [x] + [shift_both(x, sb, st) for sb, st in others]
        return [jnp.concatenate(gather(x, way), axis=0)]

    def gather_second(got, way):
        return got if way == "bt" else gather(got[0], other[way])

    half_way = {0: gather_first(block, ways[0])}
    direct_first = ways[0] == "bt"
    slots = {}
    for turn, s in enumerate(turns[1:]):
        slots[s] = shift(tie(block, half_way[0][1]) if turn >= Z_WAIT and direct_first else block, "a", s)

    local, local_lse = pl.pallas_call(
        functools.partial(resident_kernel, lay),
        out_shape=(
            jax.ShapeDtypeStruct((lay.data, LANES), jnp.float32),
            jax.ShapeDtypeStruct((-(-lay.tiles // 8) * 8, LANES), jnp.float32),
        ),
        scratch_shapes=[
            pltpu.VMEM((resident_count, lay.tiles, page, LANES), jnp.float32),
            pltpu.VMEM(own_kv.shape, jnp.float32),
        ],
        compiler_params=params(),
        name="resident",
    )(block, resident, own_kv, tie(local_counts, other_pages))

    page_count = new_pages.shape[0]
    same = routes[:, None] == routes[None, :]
    total_pages = routes.shape[0]
    earlier = lax.broadcasted_iota(jnp.int32, (total_pages, total_pages), 1) < lax.broadcasted_iota(
        jnp.int32, (total_pages, total_pages), 0
    )
    rank = jnp.sum(jnp.where(same & earlier, 1, 0), axis=1).astype(jnp.int32)
    mine = jnp.stack([routes, me * CAP + rank])
    mine = lax.dynamic_slice_in_dim(mine, tp * page_count, page_count, axis=1)
    mine = tie(mine, other_pages)
    both = jnp.stack([mine, shift(mine, "c", 1)])
    dest_a = (a_at - jnp.arange(na, dtype=jnp.int32)) % na
    dest_b = (b_at - jnp.arange(nb, dtype=jnp.int32)) % nb
    dest = (dest_a[:, None] * nb + dest_b[None, :]) * 2 + core
    hit = both[None, :, 0, None, :] == dest[:, None, :, None]
    place = lax.broadcasted_iota(jnp.int32, hit.shape, 3)
    count = jnp.sum(jnp.where(hit, 1, 0), axis=3)
    index = jnp.stack(
        [jnp.min(jnp.where(hit, place, page_count - 1), axis=3), jnp.max(jnp.where(hit, place, 0), axis=3)], axis=3
    )
    chosen = index[..., None] == lax.broadcasted_iota(jnp.int32, index.shape + (page_count,), 4)
    column = jnp.sum(jnp.where(chosen, both[None, :, 1, None, None, :], 0), axis=4)
    lists = jnp.concatenate([count[..., None], index, column], axis=3).transpose(1, 0, 2, 3).astype(jnp.int32)
    tp_of_slot = (tp - jnp.arange(nt, dtype=jnp.int32)) % nt

    own_split = new_pages.reshape(page_count, nt, heads, page, 2 * head_dim)
    other_split = other_pages.reshape(page_count, nt, heads, page, 2 * head_dim)

    def places(way):
        every = [(sb, st) for sb in range(nb) for st in range(nt)]
        if way == "bt":
            return {(sb, st): (sb * nt + st, 0) for sb, st in every}
        return {(sb, st): (st, sb) if way == "b" else (sb, st) for sb, st in every}

    def attend(s):
        query_at, result_at = places(ways[s]), places(back[s])
        counts = [0] * (1 + max(which for which, _ in result_at.values()))
        for which, _ in result_at.values():
            counts[which] += 1
        return list(
            pl.pallas_call(
                functools.partial(attend_kernel, lay, nb, nt, query_at, result_at),
                out_shape=tuple(
                    jax.ShapeDtypeStruct((count * lay.result_rows, LANES), jnp.bfloat16) for count in counts
                ),
                in_specs=[pl.BlockSpec(memory_space=pltpu.SMEM)]
                + [pl.BlockSpec(memory_space=pl.ANY)] * (len(gathered[s]) + 2),
                out_specs=(pl.BlockSpec(memory_space=pl.ANY),) * len(counts),
                scratch_shapes=[
                    pltpu.VMEM((nb, nt, lay.query_rows, LANES), jnp.bfloat16),
                    pltpu.VMEM((nb, nt, lay.result_rows, LANES), jnp.bfloat16),
                    pltpu.VMEM((nb, 2 * CAP, nt, heads, page, 2 * head_dim), jnp.bfloat16),
                    pltpu.SemaphoreType.DMA((nb, nt)),
                    pltpu.SemaphoreType.DMA((nb, nt)),
                    pltpu.SemaphoreType.DMA((nb, 2, CAP)),
                    pltpu.VMEM((2, 2 * CAP, lay.tiles, page, LANES), jnp.float32),
                    pltpu.VMEM((2 * CAP, page, LANES), jnp.float32),
                    pltpu.VMEM((lay.tail_rows, LANES), jnp.float32),
                ],
                compiler_params=params(),
                cost_estimate=pl.CostEstimate(flops=0, bytes_accessed=16 << 20, transcendentals=0),
                name="attend",
            )(jnp.concatenate([lists[:, s].reshape(-1), tp_of_slot]), *gathered[s], own_split, other_split)
        )

    def merge(arrays, blocks):
        out = jax.ShapeDtypeStruct((lay.result_rows, LANES), jnp.bfloat16)
        jobs = [(len(x), count) for x, count in zip(arrays, blocks)]
        got = pl.pallas_call(
            functools.partial(merge_kernel, lay, jobs),
            out_shape=(out,) * sum(blocks),
            scratch_shapes=[pltpu.VMEM((lay.tail_rows, LANES), jnp.float32)],
            compiler_params=params(),
            name="merge",
        )(*[x for each in arrays for x in each])
        parts = []
        for count in blocks:
            parts.append(list(got[:count]))
            got = got[count:]
        return parts

    def send_back(arrays, axis):
        return [arrays[0]] + [shift(arrays[by], axis, -by) for by in range(1, len(arrays))]

    def go_back(s):
        parts, way = first_back[s], back[s]
        if way == "bt":
            return [parts[0]] + [shift_both(parts[sb * nt + st], -sb, -st) for sb, st in others]
        parts = merge([send_back(parts, other[way])], [sizes[way]])[0]
        return send_back(parts, way)

    gathered, first_back, returned = {0: gather_second(half_way[0], ways[0])}, {}, {}
    first_back[0] = attend(0)
    for turn, s in enumerate(turns):
        if turn > 0:
            start = slots[s] if turn < R_WAIT else tie(slots[s], local_lse)
            start = start if turn < A_WAIT else tie(start, first_back[0][0])
            gathered[s] = gather_second(gather_first(start, ways[s]), ways[s])
    returned[0] = go_back(0)
    for turn, s in enumerate(turns):
        if turn > 0:
            if turn == B_WAIT:
                gathered[s][0] = tie(gathered[s][0], *returned[0][1:])
            first_back[s] = attend(s)
    arrived = list(returned[0])
    for s in turns[1:]:
        arrived.append(shift(merge([go_back(s)], [1])[0][0], "a", -s))

    return pl.pallas_call(
        functools.partial(final_kernel, lay, len(arrived)),
        out_shape=jax.ShapeDtypeStruct((requests, groups, heads, head_dim), queries.dtype),
        scratch_shapes=[
            pltpu.VMEM((lay.tail_rows, LANES), jnp.float32),
            pltpu.VMEM((requests, groups, heads, head_dim), jnp.float32),
        ],
        compiler_params=params(),
        name="final",
    )(*arrived, local, local_lse).transpose(0, 2, 1, 3)


def solution(mesh):
    return jax.shard_map(
        on_device,
        mesh=mesh,
        in_specs=(
            P(("inst", "tp"), None, None, None),
            P("inst"),
            P("inst", "tp", None, None),
            P("inst", "tp", None, None),
            P("inst", "tp", None),
            P("inst", None),
            P("inst"),
        ),
        out_specs=P("inst", "tp", None, None),
        check_vma=False,
    )
```
